256 devices in a mesh: replica: 16 (over z, core), fsdp: 16 (over x, y).
Axes of the slice: x: 4, y: 4, z: 8, core: 2. Of those that a mesh axis runs over, the one named last changes fastest.
Arguments:
- drift: bfloat16 [16, 2560, 10240], P('replica', 'fsdp'), may hold values from -12 to 12
- error: bfloat16 [16, 2560, 10240], P('replica', 'fsdp'), may hold values from -6 to 6
- start: float32 [10240, 64], replicated, may hold values from -0.0625 to 0.0625
- weights: float32 [2560, 10240], P('fsdp', 'replica'), may hold values from -3 to 3
- momentum: float32 [2560, 10240], P('fsdp', 'replica'), may hold values from -2 to 2
Outputs:
- new_weights: float32 [2560, 10240], P('fsdp', 'replica')
- new_error: bfloat16 [16, 2560, 10240], P('replica', 'fsdp')
- new_momentum: float32 [2560, 10240], P('fsdp', 'replica')
The draws below stay inside these ranges and needn't reach their ends.
All inputs are finite; a program needn't handle non-finite values.
Results may differ from the reference program's by a relative error of at most 0.001.
Values sent between devices are 32-bit elements; how exact they have to be, the bound alone decides.
No kernel may reach another device: no remote copies, remote signals or barrier semaphores. Data moves between devices by JAX's collectives and lax.ppermute only.
A program may use at most 64 MiB of HBM per device.

```python
import jax
import jax.numpy as jnp
from jax import lax

D = 2560
FF = 10240
RANK = 64
REPLICAS = 16


def with_spikes(result, stream_key, source, target, blocks, factor):
    owner, partner = [(jnp.arange(result.shape[axis_at]) // (result.shape[axis_at] // blocks)).reshape([-1 if axis == axis_at else 1 for axis in range(result.ndim)]) for axis_at in (source, target)]
    chosen = jax.random.permutation(stream_key, blocks)[partner]
    strong = (owner == chosen) | (owner == (partner + blocks // 2) % blocks)
    return jnp.where(strong, factor * result, result)


def steps_of(rng, extent, split, low, high):
    factor_of, own = 1.0, jax.random.fold_in(rng, 6)
    for axis_at, shards_of in split:
        steps = jnp.exp(jax.random.uniform(jax.random.fold_in(own, axis_at), (shards_of,), jnp.float32, low / len(split), high / len(split)))
        factor_of = factor_of * jnp.repeat(steps, extent[axis_at] // shards_of).reshape([-1 if axis == axis_at else 1 for axis in range(len(extent))])
    return factor_of


def scatter_about(stream_key, extent, deviation, most, split=(), dtype=jnp.bfloat16):
    array = deviation * jax.random.normal(stream_key, extent, jnp.float32)
    if split:
        array = array * steps_of(stream_key, extent, split, -0.22, 0.18)
    return jnp.clip(array, -most, most).astype(dtype)


def noise_with(own_key, dims, spread, limit, shards, heavy, kind=jnp.bfloat16):
    entries = spread * jax.random.normal(own_key, dims, jnp.float32)
    if shards:
        entries = entries * steps_of(own_key, dims, shards, -0.22, 0.18)
    return jnp.clip(with_spikes(entries, jax.random.fold_in(own_key, 3), *heavy), -limit, limit).astype(kind)


def setup_inputs(seed: int = 0) -> dict:
    streams_of = jax.random.split(jax.random.key(seed), 6)
    return {
        "drift": noise_with(streams_of[0], (REPLICAS, D, FF), 2.0, 12.0, ((0, 16), (1, 16)), (0, 2, 16, 2.0)),
        "error": scatter_about(streams_of[1], (REPLICAS, D, FF), 1.0, 6.0, ((0, 16), (1, 16))),
        "start": scatter_about(streams_of[2], (FF, RANK), FF ** -0.5, 0.0625, (), jnp.float32),
        "weights": scatter_about(streams_of[3], (D, FF), 0.5, 3.0, ((0, 16), (1, 16)), jnp.float32),
        "momentum": scatter_about(streams_of[4], (D, FF), 0.3, 2.0, ((0, 16), (1, 16)), jnp.float32),
    }


outer_rate = 0.7
momentum_decay = 0.9
full_prec = lax.Precision.HIGHEST

def merge_group(drift_row, error_row):
    return drift_row.astype(jnp.float32) + error_row.astype(jnp.float32)

def reference(drift, error, start, weights, momentum):
    groups = drift.shape[0]

    def left_step(total, pair):
        merged = merge_group(pair[0], pair[1])
        return (total + jnp.dot(merged.astype(jnp.float32), start.astype(jnp.float32), precision=full_prec, preferred_element_type=jnp.float32), None)
    zero_p = jnp.zeros((drift.shape[1], start.shape[1]), jnp.float32)
    sum_p, _ = lax.scan(left_step, zero_p, (drift, error))
    mean_p = sum_p / groups
    gram = jnp.dot(mean_p.T.astype(jnp.float32), mean_p.astype(jnp.float32), precision=full_prec, preferred_element_type=jnp.float32)
    lower = jnp.linalg.cholesky(gram)
    basis = lax.linalg.triangular_solve(lower, mean_p, left_side=False, lower=True, transpose_a=True)

    def right_step(total, pair):
        merged = merge_group(pair[0], pair[1])
        term = lax.dot_general(merged.astype(jnp.float32), basis.astype(jnp.float32), (((0,), (0,)), ((), ())), precision=full_prec, preferred_element_type=jnp.float32)
        return (total + term, None)
    zero_q = jnp.zeros((drift.shape[2], start.shape[1]), jnp.float32)
    sum_q, _ = lax.scan(right_step, zero_q, (drift, error))
    mean_q = sum_q / groups
    approx = lax.dot_general(basis.astype(jnp.float32), mean_q.astype(jnp.float32), (((1,), (1,)), ((), ())), precision=full_prec, preferred_element_type=jnp.float32)

    def residue(pair):
        return (merge_group(pair[0], pair[1]) - approx).astype(jnp.bfloat16)
    new_error = lax.map(residue, (drift, error))
    new_momentum = momentum_decay * momentum + approx
    new_weights = weights - outer_rate * (approx + momentum_decay * new_momentum)
    return (new_weights, new_error, new_momentum)
```

```python
import jax
import jax.numpy as jnp
from jax import lax
from jax.experimental import pallas as pl
from jax.experimental.pallas import tpu as pltpu
from jax.sharding import Mesh, PartitionSpec as P

outer_rate = 0.7
momentum_decay = 0.9

rows = 160
cols = 10240
rank = 64
wide = 1280
half_blocks = 4
blocks = 8
groups = 16
f32 = jnp.float32
bf16 = jnp.bfloat16
vmem_bytes = 40 * 1024 * 1024


def split(value, pieces):
    out = []
    for _ in range(pieces - 1):
        head = value.astype(bf16)
        out.append(head)
        value = value - head.astype(f32)
    out.append(value.astype(bf16))
    return out


def dot(a, b):
    return jnp.dot(a, b, preferred_element_type=f32)


def left_kernel(drift, error, start, out, acc):
    step = pl.program_id(0)
    both = jnp.concatenate([drift[...], error[...]], axis=0)
    factor = jnp.concatenate(split(start[...], 3), axis=1)
    term = dot(both, factor)

    @pl.when(step == 0)
    def _():
        acc[...] = term

    @pl.when(step > 0)
    def _():
        acc[...] += term

    @pl.when(step == blocks - 1)
    def _():
        total = acc[:rows, :] + acc[rows:, :]
        left = total[:, :rank] + total[:, rank : 2 * rank] + total[:, 2 * rank :]
        out[...] = jnp.concatenate([left[: rows // 2], left[rows // 2 :]], axis=1)


def left_factor(drift, error, start):
    return pl.pallas_call(
        left_kernel,
        grid=(blocks,),
        in_specs=[
            pl.BlockSpec((rows, wide), lambda s: (0, s)),
            pl.BlockSpec((rows, wide), lambda s: (0, s)),
            pl.BlockSpec((wide, rank), lambda s: (s, 0)),
        ],
        out_specs=pl.BlockSpec((rows // 2, 2 * rank), lambda s: (0, 0)),
        out_shape=jax.ShapeDtypeStruct((rows // 2, 2 * rank), f32),
        scratch_shapes=[pltpu.VMEM((2 * rows, 3 * rank), f32)],
        compiler_params=pltpu.CompilerParams(vmem_limit_bytes=vmem_bytes),
        name="left",
    )(drift, error, start)


def right_kernel(place, parts, drift, error, keep, send, left_out, pieces):
    step = pl.program_id(0)

    @pl.when(step == 0)
    def _():
        total = jnp.sum(parts[...], axis=0) * (1.0 / groups)
        left = jnp.concatenate([total[:, :rank], total[:, rank:]], axis=0)
        left_out[...] = left
        pieces[...] = jnp.concatenate(split(left.T, 3), axis=0)

    term = dot(pieces[...], drift[...]) + dot(pieces[...], error[...])
    block = term[:rank] + term[rank : 2 * rank] + term[2 * rank :]
    chunk = lax.rem(step, half_blocks)
    for x in range(4):
        part = block[16 * x : 16 * (x + 1)]

        @pl.when(step < half_blocks)
        def _():
            keep[4 * x + chunk] = part

        @pl.when(step >= half_blocks)
        def _():
            send[4 * x + chunk] = part


def column_block(step, place):
    half = step // half_blocks
    return (half + place[0] - 2 * half * place[0]) * half_blocks + lax.rem(step, half_blocks)


def right_factor(place, parts, drift, error):
    chunks = jax.ShapeDtypeStruct((16, 16, wide), f32)
    whole = pl.BlockSpec((16, 16, wide), lambda s, place: (0, 0, 0))
    return pl.pallas_call(
        right_kernel,
        grid_spec=pltpu.PrefetchScalarGridSpec(
            num_scalar_prefetch=1,
            grid=(blocks,),
            in_specs=[
                pl.BlockSpec((8, rows // 2, 2 * rank), lambda s, place: (0, 0, 0)),
                pl.BlockSpec((rows, wide), lambda s, place: (0, column_block(s, place))),
                pl.BlockSpec((rows, wide), lambda s, place: (0, column_block(s, place))),
            ],
            out_specs=[whole, whole, pl.BlockSpec((rows, rank), lambda s, place: (0, 0))],
            scratch_shapes=[pltpu.VMEM((3 * rank, rows), bf16)],
        ),
        out_shape=[chunks, chunks, jax.ShapeDtypeStruct((rows, rank), f32)],
        compiler_params=pltpu.CompilerParams(vmem_limit_bytes=vmem_bytes),
        name="right",
    )(place, parts, drift, error)


def inverse(gram):
    eye = (
        lax.broadcasted_iota(jnp.int32, (rank, rank), 0)
        == lax.broadcasted_iota(jnp.int32, (rank, rank), 1)
    ).astype(f32)
    work = jnp.concatenate([gram, eye], axis=1)
    row_id = lax.broadcasted_iota(jnp.int32, (rank, 2 * rank), 0)
    for k in range(rank):
        pivot = work[k : k + 1, :] / work[k : k + 1, k : k + 1]
        work = jnp.where(row_id == k, pivot, work - work[:, k : k + 1] * pivot)
    return work[:, rank:]


def gather_block(source, chunk):
    return jnp.concatenate([source[4 * x + chunk] for x in range(4)], axis=0)


def final_kernel(
    place, own, other, start, left, drift, error, weights, momentum,
    new_weights, new_error, new_momentum, factor, approx_buf,
):
    step = pl.program_id(0)

    @pl.when(step == 0)
    def _():
        core = place[0]
        total = jnp.zeros((3 * rank, 3 * rank), f32)
        for half, source in ((0, own), (1, other)):
            for chunk in range(half_blocks):
                block = gather_block(source, chunk)
                begin = (half + core - 2 * half * core) * (cols // 2) + chunk * wide
                basis = start[pl.ds(pl.multiple_of(begin, wide), wide), :]
                total += dot(
                    jnp.concatenate(split(block, 3), axis=0),
                    jnp.concatenate(split(basis, 3), axis=1),
                )
        total = total[:rank] + total[rank : 2 * rank] + total[2 * rank :]
        gram = (total[:, :rank] + total[:, rank : 2 * rank] + total[:, 2 * rank :]) * (1.0 / groups)
        gram = 0.5 * (gram + gram.T)
        solved = jnp.dot(
            left[...], inverse(gram) * (1.0 / groups), precision=lax.Precision.HIGHEST,
            preferred_element_type=f32,
        )
        high, low = split(solved, 2)
        factor[...] = jnp.concatenate([high, high, low], axis=1)

    chunk = lax.rem(step, half_blocks)

    def finish(source):
        high, low = split(gather_block(source, chunk), 2)
        approx = dot(factor[...], jnp.concatenate([high, low, high], axis=0))
        approx_buf[...] = approx
        merged = drift[...].astype(f32) + error[...].astype(f32)
        new_error[...] = (merged - approx).astype(bf16)

    @pl.when(step < half_blocks)
    def _():
        finish(own)

    @pl.when(step >= half_blocks)
    def _():
        finish(other)

    @pl.when(column_block(step, place) == place[1])
    def _():
        begin = pl.multiple_of(place[0] * (wide // 2), wide // 2)
        update = approx_buf[:, pl.ds(begin, wide // 2)]
        moved = momentum_decay * momentum[...] + update
        new_momentum[...] = moved
        new_weights[...] = weights[...] - outer_rate * (update + momentum_decay * moved)


def finish_step(place, own, other, start, left, drift, error, weights, momentum):
    fixed2 = lambda s, place: (0, 0)
    fixed3 = lambda s, place: (0, 0, 0)
    moving = pl.BlockSpec((rows, wide), lambda s, place: (0, column_block(s, place)))
    state = pl.BlockSpec((rows, wide // 2), fixed2)
    return pl.pallas_call(
        final_kernel,
        grid_spec=pltpu.PrefetchScalarGridSpec(
            num_scalar_prefetch=1,
            grid=(blocks,),
            in_specs=[
                pl.BlockSpec((16, 16, wide), fixed3),
                pl.BlockSpec((16, 16, wide), fixed3),
                pl.BlockSpec((cols, rank), fixed2),
                pl.BlockSpec((rows, rank), fixed2),
                moving,
                moving,
                state,
                state,
            ],
            out_specs=[state, moving, state],
            scratch_shapes=[pltpu.VMEM((rows, 3 * rank), bf16), pltpu.VMEM((rows, wide), f32)],
        ),
        out_shape=[
            jax.ShapeDtypeStruct((rows, wide // 2), f32),
            jax.ShapeDtypeStruct((rows, cols), bf16),
            jax.ShapeDtypeStruct((rows, wide // 2), f32),
        ],
        compiler_params=pltpu.CompilerParams(vmem_limit_bytes=vmem_bytes),
        name="finish",
    )(place, own, other, start, left, drift, error, weights, momentum)


def swap(value):
    return lax.ppermute(value, "core", [(0, 1), (1, 0)])


def spread(value, axes, count):
    copies = jnp.broadcast_to(value[None], (count, *value.shape))
    return lax.all_to_all(copies, axes, 0, 0)


def local(drift, error, start, weights, momentum):
    place = jnp.stack([lax.axis_index("core"), lax.axis_index("z")]).astype(jnp.int32)
    drift, error = drift[0], error[0]
    partial = left_factor(drift, error, start)
    parts = spread(partial + swap(partial), "z", 8)
    keep, send, left = right_factor(place, parts, drift, error)
    summed = lax.all_to_all(keep + swap(send), ("x", "y"), 0, 0).sum(axis=0)
    chunk = spread(summed, "z", 8).sum(axis=0)
    own = spread(chunk, ("x", "y"), 16)
    other = swap(own)
    new_weights, new_error, new_momentum = finish_step(
        place, own, other, start, left, drift, error, weights, momentum
    )
    return new_weights, new_error[None], new_momentum


def solution(mesh):
    fine = Mesh(mesh.devices.reshape(8, 2, 4, 4), ("z", "core", "x", "y"))
    replica, fsdp = ("z", "core"), ("x", "y")
    return jax.shard_map(
        local,
        mesh=fine,
        in_specs=(
            P(replica, fsdp, None),
            P(replica, fsdp, None),
            P(),
            P(fsdp, replica),
            P(fsdp, replica),
        ),
        out_specs=(P(fsdp, replica), P(replica, fsdp, None), P(fsdp, replica)),
        check_vma=False,
    )
```

```python
import jax
import jax.numpy as jnp
from jax import lax
from jax.experimental import pallas as pl
from jax.experimental.pallas import tpu as pltpu
from jax.sharding import Mesh, PartitionSpec as P

outer_rate = 0.7
momentum_decay = 0.9

rows = 160
cols = 10240
half_cols = cols // 2
rank = 64
narrow = 640
wide = 1280
blocks = 8
groups = 16
f32 = jnp.float32
bf16 = jnp.bfloat16
exact = lax.Precision.HIGHEST
mib = 1024 * 1024


def split(value, pieces):
    out = []
    for _ in range(pieces - 1):
        head = value.astype(bf16)
        out.append(head)
        value = value - head.astype(f32)
    out.append(value.astype(bf16))
    return out


def dot(a, b):
    return jnp.dot(a, b, preferred_element_type=f32)


def dot_rows(a, b):
    return lax.dot_general(a, b, (((1,), (1,)), ((), ())), preferred_element_type=f32)


def params(size):
    return pltpu.CompilerParams(vmem_limit_bytes=size * mib)


def cost(flops, moved):
    return pl.CostEstimate(flops=flops, bytes_accessed=moved, transcendentals=0)


def left_kernel(place, drift, error, start, out, send, acc):
    step = pl.program_id(0)
    both = jnp.concatenate([drift[...], error[...]], axis=0)
    factor = jnp.concatenate(split(start[...], 3), axis=0)
    term = dot_rows(both, factor)
    begin = pl.multiple_of((1 - place[0]) * narrow, narrow)
    theirs = pl.ds(begin, narrow)
    send[...] = drift[:, theirs].astype(f32) + error[:, theirs].astype(f32)

    @pl.when(step == 0)
    def _():
        acc[...] = term

    @pl.when(step > 0)
    def _():
        acc[...] += term

    @pl.when(step == blocks - 1)
    def _():
        total = acc[:rows, :] + acc[rows:, :]
        left = total[:, :rank] + total[:, rank : 2 * rank] + total[:, 2 * rank :]
        packed = jnp.concatenate([left[: rows // 2], left[rows // 2 :]], axis=1)
        for z in range(8):
            out[z] = packed


def left_factor(place, drift, error, start):
    return pl.pallas_call(
        left_kernel,
        grid_spec=pltpu.PrefetchScalarGridSpec(
            num_scalar_prefetch=1,
            grid=(blocks,),
            in_specs=[
                pl.BlockSpec((rows, wide), lambda s, place: (0, s)),
                pl.BlockSpec((rows, wide), lambda s, place: (0, s)),
                pl.BlockSpec((rank, wide), lambda s, place: (0, s)),
            ],
            out_specs=[
                pl.BlockSpec((8, rows // 2, 2 * rank), lambda s, place: (0, 0, 0)),
                pl.BlockSpec((rows, narrow), lambda s, place: (0, s)),
            ],
            scratch_shapes=[pltpu.VMEM((2 * rows, 3 * rank), f32)],
        ),
        out_shape=[
            jax.ShapeDtypeStruct((8, rows // 2, 2 * rank), f32),
            jax.ShapeDtypeStruct((rows, half_cols), f32),
        ],
        compiler_params=params(56),
        cost_estimate=cost(2 * rows * cols * rank, 13_000_000),
        name="left",
    )(place, drift, error, start)


def right_kernel(
    place, mine, theirs, drift0, drift1, error0, error1, received, out, left_out, pieces, gram
):
    step = pl.program_id(0)

    @pl.when(step == 0)
    def _():
        total = (jnp.sum(mine[...], axis=0) + jnp.sum(theirs[...], axis=0)) * (1.0 / groups)
        left = jnp.concatenate([total[:, :rank], total[:, rank:]], axis=0)
        left_out[...] = left
        turned = left.T
        pieces[...] = jnp.concatenate(split(turned, 3), axis=0)
        gram[...] = jnp.dot(turned, left, precision=exact, preferred_element_type=f32)
        own = gram[pl.ds(pl.multiple_of(place[0] * 32, 32), 32), :]
        packed = jnp.concatenate([own[:16], own[16:]], axis=1)
        for j in range(16):
            out[j, :, wide:] = packed

    first = drift0[...].astype(f32) + error0[...].astype(f32)
    second = drift1[...].astype(f32) + error1[...].astype(f32)
    merged = jnp.concatenate([first, second], axis=1) + received[...]
    high, low = split(merged, 2)
    term = dot(pieces[...], high) + dot(pieces[...], low)
    block = term[:rank] + term[rank : 2 * rank] + term[2 * rank :]
    for x in range(4):
        out[4 * x + step, :, :wide] = block[16 * x : 16 * (x + 1)]


def right_factor(place, mine, theirs, drift, error, received):
    fixed3 = lambda s, place: (0, 0, 0)
    even = pl.BlockSpec((rows, narrow), lambda s, place: (0, 4 * s + place[0]))
    odd = pl.BlockSpec((rows, narrow), lambda s, place: (0, 4 * s + 2 + place[0]))
    return pl.pallas_call(
        right_kernel,
        grid_spec=pltpu.PrefetchScalarGridSpec(
            num_scalar_prefetch=1,
            grid=(4,),
            in_specs=[
                pl.BlockSpec((8, rows // 2, 2 * rank), fixed3),
                pl.BlockSpec((8, rows // 2, 2 * rank), fixed3),
                even,
                odd,
                even,
                odd,
                pl.BlockSpec((rows, wide), lambda s, place: (0, s)),
            ],
            out_specs=[
                pl.BlockSpec((16, 16, wide + 128), fixed3),
                pl.BlockSpec((rows, rank), lambda s, place: (0, 0)),
            ],
            scratch_shapes=[pltpu.VMEM((3 * rank, rows), bf16), pltpu.VMEM((rank, rank), f32)],
        ),
        out_shape=[
            jax.ShapeDtypeStruct((16, 16, wide + 128), f32),
            jax.ShapeDtypeStruct((rows, rank), f32),
        ],
        compiler_params=params(16),
        cost_estimate=cost(2 * rows * cols * rank, 9_000_000),
        name="right",
    )(place, mine, theirs, drift, drift, error, error, received)


def inverse(gram):
    eye = (
        lax.broadcasted_iota(jnp.int32, (rank, rank), 0)
        == lax.broadcasted_iota(jnp.int32, (rank, rank), 1)
    ).astype(f32)
    work = jnp.concatenate([gram, eye], axis=1)
    row_id = lax.broadcasted_iota(jnp.int32, (rank, 2 * rank), 0)
    for k in range(rank):
        pivot = work[k : k + 1, :] / work[k : k + 1, k : k + 1]
        work = jnp.where(row_id == k, pivot, work - work[:, k : k + 1] * pivot)
    return work[:, rank:]


def solve_kernel(place, mine, theirs, left, out):
    def unpack(packed):
        return jnp.concatenate([packed[:, :rank], packed[:, rank:]], axis=0)

    own, other = unpack(mine[...]), unpack(theirs[...])
    first = place[0] == 0
    gram = jnp.concatenate([jnp.where(first, own, other), jnp.where(first, other, own)], axis=0)
    solved = jnp.dot(
        left[...], inverse(gram) * (1.0 / groups), precision=exact, preferred_element_type=f32
    )
    high, low = split(solved, 2)
    out[...] = jnp.concatenate([high, high, low], axis=1)


def solve(place, mine, theirs, left):
    vmem = pl.BlockSpec(memory_space=pltpu.VMEM)
    return pl.pallas_call(
        solve_kernel,
        in_specs=[pl.BlockSpec(memory_space=pltpu.SMEM), vmem, vmem, vmem],
        out_specs=vmem,
        out_shape=jax.ShapeDtypeStruct((rows, 3 * rank), bf16),
        compiler_params=params(8),
        cost_estimate=cost(0, 30_000_000),
        name="solve",
    )(place, mine, theirs, left)


def apply_factor(factor, right, drift, error, new_error):
    step = pl.program_id(0)
    y, odd = step // 2, lax.rem(step, 2)
    lanes = pl.ds(pl.multiple_of(odd * narrow, narrow), narrow)
    block = jnp.concatenate([right[4 * x + y, :, lanes] for x in range(4)], axis=0)
    high, low = split(block, 2)
    approx = dot(factor[...], jnp.concatenate([high, low, high], axis=0))
    merged = drift[...].astype(f32) + error[...].astype(f32)
    new_error[...] = (merged - approx).astype(bf16)
    return approx


def own_kernel(
    place, factor, right, drift, error, weights, momentum, new_error, new_weights, new_momentum
):
    approx = apply_factor(factor, right, drift, error, new_error)

    @pl.when(pl.program_id(0) == place[1])
    def _():
        moved = momentum_decay * momentum[...] + approx
        new_momentum[...] = moved
        new_weights[...] = weights[...] - outer_rate * (approx + momentum_decay * moved)


def other_kernel(place, factor, right, drift, error, partial, new_error):
    apply_factor(factor, right, drift, error, new_error)


fixed2 = lambda s, place: (0, 0)
fixed3 = lambda s, place: (0, 0, 0)


def finish_own(place, factor, right, drift, error, weights, momentum):
    block = pl.BlockSpec((rows, narrow), lambda s, place: (0, 2 * s + place[0]))
    state = pl.BlockSpec((rows, narrow), fixed2)
    return pl.pallas_call(
        own_kernel,
        grid_spec=pltpu.PrefetchScalarGridSpec(
            num_scalar_prefetch=1,
            grid=(blocks,),
            in_specs=[
                pl.BlockSpec((rows, 3 * rank), fixed2),
                pl.BlockSpec((16, 16, wide), fixed3),
                block,
                block,
                state,
                state,
            ],
            out_specs=[block, state, state],
        ),
        out_shape=[
            jax.ShapeDtypeStruct((rows, cols), bf16),
            jax.ShapeDtypeStruct((rows, narrow), f32),
            jax.ShapeDtypeStruct((rows, narrow), f32),
        ],
        compiler_params=params(16),
        cost_estimate=cost(rows * cols * rank, 8_000_000),
        name="own",
    )(place, factor, right, drift, error, weights, momentum)


def finish_other(place, factor, right, drift, error, partial):
    block = pl.BlockSpec((rows, narrow), lambda s, place: (0, 2 * s + 1 - place[0]))
    return pl.pallas_call(
        other_kernel,
        grid_spec=pltpu.PrefetchScalarGridSpec(
            num_scalar_prefetch=1,
            grid=(blocks,),
            in_specs=[
                pl.BlockSpec((rows, 3 * rank), fixed2),
                pl.BlockSpec((16, 16, wide), fixed3),
                block,
                block,
                pl.BlockSpec(memory_space=pl.ANY),
            ],
            out_specs=block,
        ),
        out_shape=jax.ShapeDtypeStruct((rows, cols), bf16),
        input_output_aliases={5: 0},
        compiler_params=params(16),
        cost_estimate=cost(rows * cols * rank, 8_000_000),
        name="other",
    )(place, factor, right, drift, error, partial)


def swap(value):
    return lax.ppermute(value, "core", [(0, 1), (1, 0)])


def spread(value, axes, count):
    copies = jnp.broadcast_to(value[None], (count, *value.shape))
    return lax.all_to_all(copies, axes, 0, 0)


def local(drift, error, start, weights, momentum):
    place = jnp.stack([lax.axis_index("core"), lax.axis_index("z")]).astype(jnp.int32)
    drift, error = drift[0], error[0]
    copies, sent = left_factor(place, drift, error, start.T)
    received = swap(sent)
    mine = lax.all_to_all(copies, "z", 0, 0)
    chunks, left = right_factor(place, mine, swap(mine), drift, error, received)
    summed = lax.all_to_all(chunks, ("x", "y"), 0, 0).sum(axis=0)
    gram = summed[:, wide:]
    factor = solve(place, gram, swap(gram), left)
    chunk = spread(summed[:, :wide], "z", 8).sum(axis=0)
    own = spread(chunk, ("x", "y"), 16)
    other = swap(own)
    partial, new_weights, new_momentum = finish_own(
        place, factor, own, drift, error, weights, momentum
    )
    new_error = finish_other(place, factor, other, drift, error, partial)
    return new_weights, new_error[None], new_momentum


def solution(mesh):
    fine = Mesh(mesh.devices.reshape(8, 2, 4, 4), ("z", "core", "x", "y"))
    replica, fsdp = ("z", "core"), ("x", "y")
    return jax.shard_map(
        local,
        mesh=fine,
        in_specs=(
            P(replica, fsdp, None),
            P(replica, fsdp, None),
            P(),
            P(fsdp, replica),
            P(fsdp, replica),
        ),
        out_specs=(P(fsdp, replica), P(replica, fsdp, None), P(fsdp, replica)),
        check_vma=False,
    )
```

```python
import jax
import jax.numpy as jnp
from jax import lax
from jax.experimental import pallas as pl
from jax.experimental.pallas import tpu as pltpu
from jax.sharding import Mesh, PartitionSpec as P

outer_rate = 0.7
momentum_decay = 0.9

rows = 160
cols = 10240
rank = 64
narrow = 640
wide = 1280
blocks = 8
groups = 16
tall = 160
f32 = jnp.float32
bf16 = jnp.bfloat16
exact = lax.Precision.HIGHEST
mib = 1024 * 1024
hbm = pl.BlockSpec(memory_space=pltpu.HBM)
vmem = pl.BlockSpec(memory_space=pltpu.VMEM)


def split(value, pieces):
    out = []
    for _ in range(pieces - 1):
        head = value.astype(bf16)
        out.append(head)
        value = value - head.astype(f32)
    out.append(value.astype(bf16))
    return out


def dot(a, b):
    return jnp.dot(a, b, preferred_element_type=f32)


def dot_rows(a, b):
    return lax.dot_general(a, b, (((1,), (1,)), ((), ())), preferred_element_type=f32)


def call(kernel, name, size, moved, **kwargs):
    return pl.pallas_call(
        kernel,
        name=name,
        compiler_params=pltpu.CompilerParams(vmem_limit_bytes=size * mib),
        cost_estimate=pl.CostEstimate(flops=0, bytes_accessed=moved, transcendentals=0),
        **kwargs,
    )


def shape(*dims, dtype=f32):
    return jax.ShapeDtypeStruct(dims, dtype)


def left_kernel(drift, error, start, out, keep, send, drifts, errors, starts, acc, sems):
    first = lax.axis_index("core") == 0
    copies = []
    for i in range(blocks):
        lanes = pl.ds(i * wide, wide)
        mine = [
            pltpu.make_async_copy(start.at[:, lanes], starts.at[i], sems.at[i, 0]),
            pltpu.make_async_copy(drift.at[:, lanes], drifts.at[i], sems.at[i, 1]),
            pltpu.make_async_copy(error.at[:, lanes], errors.at[i], sems.at[i, 2]),
        ]
        for copy in mine:
            copy.start()
        copies.append(mine)
    for i in range(blocks):
        for copy in copies[i]:
            copy.wait()
        both = jnp.concatenate([drifts[i], errors[i]], axis=0)
        factor = jnp.concatenate(split(starts[i], 3), axis=0)
        term = dot_rows(both, factor)
        if i == 0:
            acc[...] = term
        else:
            acc[...] += term
        merged = drifts[i].astype(f32) + errors[i].astype(f32)
        even, odd = merged[:, :narrow], merged[:, narrow:]
        keep[i] = jnp.where(first, even, odd)
        send[i] = jnp.where(first, odd, even)
    total = acc[:rows, :] + acc[rows:, :]
    left = total[:, :rank] + total[:, rank : 2 * rank] + total[:, 2 * rank :]
    packed = jnp.concatenate([left[: rows // 2], left[rows // 2 :]], axis=1)
    for z in range(8):
        out[z] = packed


def left_factor(drift, error, start):
    return call(
        left_kernel, "left", 24, 13_000_000,
        in_specs=[hbm, hbm, hbm],
        out_specs=[vmem, vmem, vmem],
        out_shape=[
            pltpu.VMEM((8, rows // 2, 2 * rank), f32),
            pltpu.VMEM((blocks, rows, narrow), f32),
            pltpu.VMEM((blocks, rows, narrow), f32),
        ],
        scratch_shapes=[
            pltpu.VMEM((blocks, rows, wide), bf16),
            pltpu.VMEM((blocks, rows, wide), bf16),
            pltpu.VMEM((blocks, rank, wide), f32),
            pltpu.VMEM((2 * rows, 3 * rank), f32),
            pltpu.SemaphoreType.DMA((blocks, 3)),
        ],
    )(*[pltpu.with_memory_space_constraint(value, pltpu.HBM) for value in (drift, error, start)])


def right_kernel(mine, theirs, keep, received, out, left_out, gram):
    total = (jnp.sum(mine[...], axis=0) + jnp.sum(theirs[...], axis=0)) * (1.0 / groups)
    left = jnp.concatenate([total[:, :rank], total[:, rank:]], axis=0)
    left_out[...] = left
    turned = left.T
    pieces = jnp.concatenate(split(turned, 3), axis=0)
    gram[...] = jnp.dot(turned, left, precision=exact, preferred_element_type=f32)
    own = gram[pl.ds(pl.multiple_of(lax.axis_index("core") * 32, 32), 32), :]
    packed = jnp.concatenate([own[:16], own[16:]], axis=1)
    for j in range(16):
        out[j, tall:, :] = packed
    for y in range(4):
        for part in range(2):
            k = 2 * y + part
            high, low = split(keep[k] + received[k], 2)
            term = dot(pieces, high) + dot(pieces, low)
            block = term[:rank] + term[rank : 2 * rank] + term[2 * rank :]
            for x in range(4):
                for t in range(5):
                    begin = 16 * (5 * part + t)
                    out[4 * x + y, begin : begin + 16, :] = block[
                        16 * x : 16 * (x + 1), 128 * t : 128 * (t + 1)
                    ]


def right_factor(mine, theirs, keep, received):
    return call(
        right_kernel, "right", 16, 10_000_000,
        in_specs=[vmem] * 4,
        out_specs=[vmem, vmem],
        out_shape=[shape(16, tall + 16, 128), shape(rows, rank)],
        scratch_shapes=[pltpu.VMEM((rank, rank), f32)],
    )(mine, theirs, keep, received)


def plane_sum_kernel(chunks, out, gram):
    total = chunks[0]
    for j in range(1, 16):
        total += chunks[j]
    gram[...] = total[tall:]
    for z in range(8):
        out[z] = total[:tall]


def plane_sum(chunks):
    return call(
        plane_sum_kernel, "plane_sum", 8, 3_000_000,
        in_specs=[vmem],
        out_specs=[vmem, vmem],
        out_shape=[shape(8, tall, 128), shape(16, 128)],
    )(chunks)


def line_sum_kernel(chunks, out):
    total = chunks[0]
    for j in range(1, 8):
        total += chunks[j]
    for j in range(16):
        out[j] = total


def line_sum(chunks):
    return call(
        line_sum_kernel, "line_sum", 8, 3_000_000,
        in_specs=[vmem],
        out_specs=vmem,
        out_shape=shape(16, tall, 128),
    )(chunks)


def inverse(gram):
    eye = (
        lax.broadcasted_iota(jnp.int32, (rank, rank), 0)
        == lax.broadcasted_iota(jnp.int32, (rank, rank), 1)
    ).astype(f32)
    work = jnp.concatenate([gram, eye], axis=1)
    row_id = lax.broadcasted_iota(jnp.int32, (rank, 2 * rank), 0)
    for k in range(rank):
        pivot = work[k : k + 1, :] / work[k : k + 1, k : k + 1]
        work = jnp.where(row_id == k, pivot, work - work[:, k : k + 1] * pivot)
    return work[:, rank:]


def solve_kernel(mine, theirs, left, out):
    def unpack(packed):
        return jnp.concatenate([packed[:, :rank], packed[:, rank:]], axis=0)

    own, other = unpack(mine[...]), unpack(theirs[...])
    first = lax.axis_index("core") == 0
    gram = jnp.concatenate([jnp.where(first, own, other), jnp.where(first, other, own)], axis=0)
    solved = jnp.dot(
        left[...], inverse(gram) * (1.0 / groups), precision=exact, preferred_element_type=f32
    )
    high, low = split(solved, 2)
    out[...] = jnp.concatenate([high, high, low], axis=1)


def solve(mine, theirs, left):
    return call(
        solve_kernel, "solve", 8, 20_000_000,
        in_specs=[vmem] * 3,
        out_specs=vmem,
        out_shape=shape(rows, 3 * rank, dtype=bf16),
    )(mine, theirs, left)


def block_copy(k, offset, held, new_error, sems):
    begin = pl.multiple_of((2 * k + offset) * narrow, narrow)
    return pltpu.make_async_copy(held.at[k], new_error.at[:, pl.ds(begin, narrow)], sems.at[k])


def approx_block(k, factor, right):
    y, part = k // 2, k % 2
    tiles = []
    for t in range(5):
        begin = 16 * (5 * part + t)
        tiles.append(
            jnp.concatenate([right[4 * x + y, begin : begin + 16, :] for x in range(4)], axis=0)
        )
    high, low = split(jnp.concatenate(tiles, axis=1), 2)
    return dot(factor, jnp.concatenate([high, low, high], axis=0))


def own_kernel(
    factor, right, merged, weights, momentum, new_error, new_weights, new_momentum,
    held, held_weights, held_momentum, sems, state_sems,
):
    core, z = lax.axis_index("core"), lax.axis_index("z")
    left = factor[...]
    copies = []
    state = [
        pltpu.make_async_copy(held_weights, new_weights, state_sems.at[0]),
        pltpu.make_async_copy(held_momentum, new_momentum, state_sems.at[1]),
    ]
    for k in range(blocks):
        approx = approx_block(k, left, right)
        held[k] = (merged[k] - approx).astype(bf16)
        copies.append(block_copy(k, core, held, new_error, sems))
        copies[-1].start()

        @pl.when(z == k)
        def _():
            moved = momentum_decay * momentum[...] + approx
            held_momentum[...] = moved
            held_weights[...] = weights[...] - outer_rate * (approx + momentum_decay * moved)

    for copy in state:
        copy.start()
    for copy in copies + state:
        copy.wait()


def finish_own(factor, right, merged, weights, momentum):
    return call(
        own_kernel, "own", 16, 8_000_000,
        in_specs=[vmem] * 5,
        out_specs=[hbm, hbm, hbm],
        out_shape=[shape(rows, cols, dtype=bf16), shape(rows, narrow), shape(rows, narrow)],
        scratch_shapes=[
            pltpu.VMEM((blocks, rows, narrow), bf16),
            pltpu.VMEM((rows, narrow), f32),
            pltpu.VMEM((rows, narrow), f32),
            pltpu.SemaphoreType.DMA((blocks,)),
            pltpu.SemaphoreType.DMA((2,)),
        ],
    )(factor, right, merged, weights, momentum)


def other_kernel(factor, right, merged, partial, new_error, held, sems):
    offset = 1 - lax.axis_index("core")
    left = factor[...]
    copies = []
    for k in range(blocks):
        held[k] = (merged[k] - approx_block(k, left, right)).astype(bf16)
        copies.append(block_copy(k, offset, held, new_error, sems))
        copies[-1].start()
    for copy in copies:
        copy.wait()


def finish_other(factor, right, merged, partial):
    return call(
        other_kernel, "other", 16, 8_000_000,
        in_specs=[vmem, vmem, vmem, hbm],
        out_specs=hbm,
        out_shape=shape(rows, cols, dtype=bf16),
        input_output_aliases={3: 0},
        scratch_shapes=[
            pltpu.VMEM((blocks, rows, narrow), bf16),
            pltpu.SemaphoreType.DMA((blocks,)),
        ],
    )(factor, right, merged, partial)


def swap(value):
    return lax.ppermute(value, "core", [(0, 1), (1, 0)])


def local(drift, error, start, weights, momentum):
    copies, keep, send = left_factor(drift[0], error[0], start.T)
    received = swap(send)
    mine = lax.all_to_all(copies, "z", 0, 0)
    chunks, left = right_factor(mine, swap(mine), keep, received)
    plane, gram = plane_sum(lax.all_to_all(chunks, ("x", "y"), 0, 0))
    factor = solve(gram, swap(gram), left)
    line = lax.all_to_all(plane, "z", 0, 0)
    line, factor = lax.optimization_barrier((line, factor))
    own = lax.all_to_all(line_sum(line), ("x", "y"), 0, 0)
    other = swap(own)
    partial, new_weights, new_momentum = finish_own(factor, own, keep, weights, momentum)
    new_error = finish_other(factor, other, send, partial)
    return new_weights, new_error[None], new_momentum


def solution(mesh):
    fine = Mesh(mesh.devices.reshape(8, 2, 4, 4), ("z", "core", "x", "y"))
    replica, fsdp = ("z", "core"), ("x", "y")
    return jax.shard_map(
        local,
        mesh=fine,
        in_specs=(
            P(replica, fsdp, None),
            P(replica, fsdp, None),
            P(),
            P(fsdp, replica),
            P(fsdp, replica),
        ),
        out_specs=(P(fsdp, replica), P(replica, fsdp, None), P(fsdp, replica)),
        check_vma=False,
    )
```

```python
import jax
import jax.numpy as jnp
from jax import lax
from jax.experimental import pallas as pl
from jax.experimental.pallas import tpu as pltpu
from jax.sharding import Mesh, PartitionSpec as P

outer_rate = 0.7
momentum_decay = 0.9

rows = 160
cols = 10240
rank = 64
narrow = 640
wide = 1280
blocks = 8
groups = 16
tall = 160
f32 = jnp.float32
bf16 = jnp.bfloat16
exact = lax.Precision.HIGHEST
mib = 1024 * 1024
hbm = pl.BlockSpec(memory_space=pltpu.HBM)
vmem = pl.BlockSpec(memory_space=pltpu.VMEM)


def split(value, pieces):
    out = []
    for _ in range(pieces - 1):
        head = value.astype(bf16)
        out.append(head)
        value = value - head.astype(f32)
    out.append(value.astype(bf16))
    return out


def dot(a, b):
    return jnp.dot(a, b, preferred_element_type=f32)


def dot_rows(a, b):
    return lax.dot_general(a, b, (((1,), (1,)), ((), ())), preferred_element_type=f32)


def call(kernel, name, size, moved, **kwargs):
    return pl.pallas_call(
        kernel,
        name=name,
        compiler_params=pltpu.CompilerParams(vmem_limit_bytes=size * mib),
        cost_estimate=pl.CostEstimate(flops=0, bytes_accessed=moved, transcendentals=0),
        **kwargs,
    )


def shape(*dims, dtype=f32):
    return jax.ShapeDtypeStruct(dims, dtype)


def left_kernel(drift, error, start, out, keep, send, drifts, errors, starts, acc, sems):
    first = lax.axis_index("core") == 0
    copies = []
    for i in range(blocks):
        lanes = pl.ds(i * wide, wide)
        mine = [
            pltpu.make_async_copy(start.at[:, lanes], starts.at[i], sems.at[i, 0]),
            pltpu.make_async_copy(drift.at[:, lanes], drifts.at[i], sems.at[i, 1]),
            pltpu.make_async_copy(error.at[:, lanes], errors.at[i], sems.at[i, 2]),
        ]
        for copy in mine:
            copy.start()
        copies.append(mine)
    for i in range(blocks):
        for copy in copies[i]:
            copy.wait()
        both = jnp.concatenate([drifts[i], errors[i]], axis=0)
        factor = jnp.concatenate(split(starts[i], 3), axis=0)
        term = dot_rows(both, factor)
        if i == 0:
            acc[...] = term
        else:
            acc[...] += term
        merged = drifts[i].astype(f32) + errors[i].astype(f32)
        even, odd = merged[:, :narrow], merged[:, narrow:]
        keep[i] = jnp.where(first, even, odd)
        send[i] = jnp.where(first, odd, even)
    total = acc[:rows, :] + acc[rows:, :]
    left = total[:, :rank] + total[:, rank : 2 * rank] + total[:, 2 * rank :]
    packed = jnp.concatenate([left[: rows // 2], left[rows // 2 :]], axis=1)
    for z in range(8):
        out[z] = packed


def left_factor(drift, error, start):
    return call(
        left_kernel, "left", 24, 13_000_000,
        in_specs=[hbm, hbm, hbm],
        out_specs=[vmem, vmem, vmem],
        out_shape=[
            pltpu.VMEM((8, rows // 2, 2 * rank), f32),
            pltpu.VMEM((blocks, rows, narrow), f32),
            pltpu.VMEM((blocks, rows, narrow), f32),
        ],
        scratch_shapes=[
            pltpu.VMEM((blocks, rows, wide), bf16),
            pltpu.VMEM((blocks, rows, wide), bf16),
            pltpu.VMEM((blocks, rank, wide), f32),
            pltpu.VMEM((2 * rows, 3 * rank), f32),
            pltpu.SemaphoreType.DMA((blocks, 3)),
        ],
    )(*[pltpu.with_memory_space_constraint(value, pltpu.HBM) for value in (drift, error, start)])


def right_kernel(mine, theirs, keep, received, out, left_out, gram):
    total = (jnp.sum(mine[...], axis=0) + jnp.sum(theirs[...], axis=0)) * (1.0 / groups)
    left = jnp.concatenate([total[:, :rank], total[:, rank:]], axis=0)
    left_out[...] = left
    turned = left.T
    pieces = jnp.concatenate(split(turned, 3), axis=0)
    gram[...] = jnp.dot(turned, left, precision=exact, preferred_element_type=f32)
    share = gram[pl.ds(pl.multiple_of(lax.axis_index("z") * 8, 8), 8), :]
    padded = jnp.concatenate([share, jnp.zeros((8, rank), f32)], axis=1)
    for j in range(16):
        out[j, tall:, :] = padded
    for y in range(4):
        for part in range(2):
            k = 2 * y + part
            high, low = split(keep[k] + received[k], 2)
            term = dot(pieces, high) + dot(pieces, low)
            block = term[:rank] + term[rank : 2 * rank] + term[2 * rank :]
            for x in range(4):
                for t in range(5):
                    begin = 16 * (5 * part + t)
                    out[4 * x + y, begin : begin + 16, :] = block[
                        16 * x : 16 * (x + 1), 128 * t : 128 * (t + 1)
                    ]


def right_factor(mine, theirs, keep, received):
    return call(
        right_kernel, "right", 16, 10_000_000,
        in_specs=[vmem] * 4,
        out_specs=[vmem, vmem],
        out_shape=[shape(16, tall + 8, 128), shape(rows, rank)],
        scratch_shapes=[pltpu.VMEM((rank, rank), f32)],
    )(mine, theirs, keep, received)


def plane_sum_kernel(chunks, out):
    total = chunks[0]
    for j in range(1, 16):
        total += chunks[j]
    for z in range(8):
        out[z] = total


def plane_sum(chunks):
    return call(
        plane_sum_kernel, "plane_sum", 8, 3_000_000,
        in_specs=[vmem],
        out_specs=vmem,
        out_shape=shape(8, tall + 8, 128),
    )(chunks)


def line_sum_kernel(chunks, out, gram):
    total = chunks[0, :tall, :]
    for j in range(1, 8):
        total += chunks[j, :tall, :]
    for j in range(16):
        out[j] = total
    for j in range(8):
        gram[8 * j : 8 * (j + 1), :] = chunks[j, tall:, :]


def line_sum(chunks):
    return call(
        line_sum_kernel, "line_sum", 8, 3_000_000,
        in_specs=[vmem],
        out_specs=[vmem, vmem],
        out_shape=[shape(16, tall, 128), shape(rank, 2 * rank)],
    )(chunks)


def inverse(gram):
    size = (rank, 2 * rank)
    row = lax.broadcasted_iota(jnp.int32, size, 0)
    work = jnp.where(lax.broadcasted_iota(jnp.int32, size, 1) == row + rank, 1.0, gram)
    step = 8
    for k in range(0, rank, step):
        columns = [jnp.broadcast_to(work[:, k + j : k + j + 1], size) for j in range(step)]
        block = [[columns[j][k + i : k + i + 1, :] for j in range(step)] for i in range(step)]
        pivots = [work[k + i : k + i + 1, :] for i in range(step)]
        for j in range(step):
            scale = 1.0 / block[j][j]
            pivots[j] = pivots[j] * scale
            for m in range(j + 1, step):
                block[j][m] = block[j][m] * scale
            for i in range(step):
                if i != j:
                    pivots[i] = pivots[i] - block[i][j] * pivots[j]
                    for m in range(j + 1, step):
                        block[i][m] = block[i][m] - block[i][j] * block[j][m]
        for j in range(step):
            work = work - columns[j] * pivots[j]
        for j in range(step):
            work = jnp.where(row == k + j, pivots[j], work)
    return work[:, rank:]


def solve(gram, left):
    solved = jnp.dot(
        left, inverse(gram) * (1.0 / groups), precision=exact, preferred_element_type=f32
    )
    high, low = split(solved, 2)
    return jnp.concatenate([high, high, low], axis=1)


def block_copy(k, offset, held, new_error, sems):
    begin = pl.multiple_of((2 * k + offset) * narrow, narrow)
    return pltpu.make_async_copy(held.at[k], new_error.at[:, pl.ds(begin, narrow)], sems.at[k])


def approx_block(k, factor, right):
    y, part = k // 2, k % 2
    tiles = []
    for t in range(5):
        begin = 16 * (5 * part + t)
        tiles.append(
            jnp.concatenate([right[4 * x + y, begin : begin + 16, :] for x in range(4)], axis=0)
        )
    high, low = split(jnp.concatenate(tiles, axis=1), 2)
    return dot(factor, jnp.concatenate([high, low, high], axis=0))


def own_kernel(
    gram, left, right, merged, weights, momentum, new_error, new_weights, new_momentum, factor,
    held, held_weights, held_momentum, sems, state_sems,
):
    core, z = lax.axis_index("core"), lax.axis_index("z")
    solved = solve(gram[...], left[...])
    factor[...] = solved
    copies = []
    state = [
        pltpu.make_async_copy(held_weights, new_weights, state_sems.at[0]),
        pltpu.make_async_copy(held_momentum, new_momentum, state_sems.at[1]),
    ]
    for k in range(blocks):
        approx = approx_block(k, solved, right)
        held[k] = (merged[k] - approx).astype(bf16)
        copies.append(block_copy(k, core, held, new_error, sems))
        copies[-1].start()

        @pl.when(z == k)
        def _():
            moved = momentum_decay * momentum[...] + approx
            held_momentum[...] = moved
            held_weights[...] = weights[...] - outer_rate * (approx + momentum_decay * moved)

    for copy in state:
        copy.start()
    for copy in copies + state:
        copy.wait()


def finish_own(gram, left, right, merged, weights, momentum):
    return call(
        own_kernel, "own", 16, 16_000_000,
        in_specs=[vmem] * 6,
        out_specs=[hbm, hbm, hbm, vmem],
        out_shape=[
            shape(rows, cols, dtype=bf16),
            shape(rows, narrow),
            shape(rows, narrow),
            shape(rows, 3 * rank, dtype=bf16),
        ],
        scratch_shapes=[
            pltpu.VMEM((blocks, rows, narrow), bf16),
            pltpu.VMEM((rows, narrow), f32),
            pltpu.VMEM((rows, narrow), f32),
            pltpu.SemaphoreType.DMA((blocks,)),
            pltpu.SemaphoreType.DMA((2,)),
        ],
    )(gram, left, right, merged, weights, momentum)


def other_kernel(factor, right, merged, partial, new_error, held, sems):
    offset = 1 - lax.axis_index("core")
    left = factor[...]
    copies = []
    for k in range(blocks):
        held[k] = (merged[k] - approx_block(k, left, right)).astype(bf16)
        copies.append(block_copy(k, offset, held, new_error, sems))
        copies[-1].start()
    for copy in copies:
        copy.wait()


def finish_other(factor, right, merged, partial):
    return call(
        other_kernel, "other", 16, 8_000_000,
        in_specs=[vmem, vmem, vmem, hbm],
        out_specs=hbm,
        out_shape=shape(rows, cols, dtype=bf16),
        input_output_aliases={3: 0},
        scratch_shapes=[
            pltpu.VMEM((blocks, rows, narrow), bf16),
            pltpu.SemaphoreType.DMA((blocks,)),
        ],
    )(factor, right, merged, partial)


def swap(value):
    return lax.ppermute(value, "core", [(0, 1), (1, 0)])


def local(drift, error, start, weights, momentum):
    copies, keep, send = left_factor(drift[0], error[0], start.T)
    received = swap(send)
    mine = lax.all_to_all(copies, "z", 0, 0)
    chunks, left = right_factor(mine, swap(mine), keep, received)
    plane = plane_sum(lax.all_to_all(chunks, ("x", "y"), 0, 0))
    line, gram = line_sum(lax.all_to_all(plane, "z", 0, 0))
    own = lax.all_to_all(line, ("x", "y"), 0, 0)
    other = swap(own)
    partial, new_weights, new_momentum, factor = finish_own(
        gram, left, own, keep, weights, momentum
    )
    new_error = finish_other(factor, other, send, partial)
    return new_weights, new_error[None], new_momentum


def solution(mesh):
    fine = Mesh(mesh.devices.reshape(8, 2, 4, 4), ("z", "core", "x", "y"))
    replica, fsdp = ("z", "core"), ("x", "y")
    return jax.shard_map(
        local,
        mesh=fine,
        in_specs=(
            P(replica, fsdp, None),
            P(replica, fsdp, None),
            P(),
            P(fsdp, replica),
            P(fsdp, replica),
        ),
        out_specs=(P(fsdp, replica), P(replica, fsdp, None), P(fsdp, replica)),
        check_vma=False,
    )
```

```python
import jax
import jax.numpy as jnp
from jax import lax
from jax.experimental import pallas as pl
from jax.experimental.pallas import tpu as pltpu
from jax.sharding import Mesh, PartitionSpec as P

outer_rate = 0.7
momentum_decay = 0.9

rows = 160
cols = 10240
rank = 64
narrow = 640
wide = 1280
blocks = 8
groups = 16
tall = 80
f32 = jnp.float32
bf16 = jnp.bfloat16
exact = lax.Precision.HIGHEST
mib = 1024 * 1024
hbm = pl.BlockSpec(memory_space=pltpu.HBM)
vmem = pl.BlockSpec(memory_space=pltpu.VMEM)


def split(value, pieces):
    out = []
    for _ in range(pieces - 1):
        head = value.astype(bf16)
        out.append(head)
        value = value - head.astype(f32)
    out.append(value.astype(bf16))
    return out


def dot(a, b):
    return jnp.dot(a, b, preferred_element_type=f32)


def dot_rows(a, b):
    return lax.dot_general(a, b, (((1,), (1,)), ((), ())), preferred_element_type=f32)


def call(kernel, name, size, moved, **kwargs):
    return pl.pallas_call(
        kernel,
        name=name,
        compiler_params=pltpu.CompilerParams(vmem_limit_bytes=size * mib),
        cost_estimate=pl.CostEstimate(flops=0, bytes_accessed=moved, transcendentals=0),
        **kwargs,
    )


def shape(*dims, dtype=f32):
    return jax.ShapeDtypeStruct(dims, dtype)


def left_kernel(drift, error, start, out, keep, send, drifts, errors, starts, acc, sems):
    first = lax.axis_index("core") == 0
    copies = []
    for i in range(blocks):
        lanes = pl.ds(i * wide, wide)
        mine = [
            pltpu.make_async_copy(start.at[:, lanes], starts.at[i], sems.at[i, 0]),
            pltpu.make_async_copy(drift.at[:, lanes], drifts.at[i], sems.at[i, 1]),
            pltpu.make_async_copy(error.at[:, lanes], errors.at[i], sems.at[i, 2]),
        ]
        for copy in mine:
            copy.start()
        copies.append(mine)
    for i in range(blocks):
        for copy in copies[i]:
            copy.wait()
        both = jnp.concatenate([drifts[i], errors[i]], axis=0)
        factor = jnp.concatenate(split(starts[i], 3), axis=0)
        term = dot_rows(both, factor)
        if i == 0:
            acc[...] = term
        else:
            acc[...] += term
        merged = drifts[i].astype(f32) + errors[i].astype(f32)
        even, odd = merged[:, :narrow], merged[:, narrow:]
        keep[i] = jnp.where(first, even, odd)
        send[i] = jnp.where(first, odd, even)
    total = acc[:rows, :] + acc[rows:, :]
    left = total[:, :rank] + total[:, rank : 2 * rank] + total[:, 2 * rank :]
    packed = jnp.concatenate([left[: rows // 2], left[rows // 2 :]], axis=1)
    for z in range(8):
        out[z] = packed


def left_factor(drift, error, start):
    return call(
        left_kernel, "left", 24, 13_000_000,
        in_specs=[hbm, hbm, hbm],
        out_specs=[vmem, vmem, vmem],
        out_shape=[
            pltpu.VMEM((8, rows // 2, 2 * rank), f32),
            pltpu.VMEM((blocks, rows, narrow), f32),
            pltpu.VMEM((blocks, rows, narrow), f32),
        ],
        scratch_shapes=[
            pltpu.VMEM((blocks, rows, wide), bf16),
            pltpu.VMEM((blocks, rows, wide), bf16),
            pltpu.VMEM((blocks, rank, wide), f32),
            pltpu.VMEM((2 * rows, 3 * rank), f32),
            pltpu.SemaphoreType.DMA((blocks, 3)),
        ],
    )(*[pltpu.with_memory_space_constraint(value, pltpu.HBM) for value in (drift, error, start)])


def line_index():
    return 2 * lax.axis_index("zh") + lax.axis_index("zl")


def right_kernel(mine, theirs, keep, received, out, left_out, gram):
    total = (jnp.sum(mine[...], axis=0) + jnp.sum(theirs[...], axis=0)) * (1.0 / groups)
    left = jnp.concatenate([total[:, :rank], total[:, rank:]], axis=0)
    left_out[...] = left
    turned = left.T
    pieces = jnp.concatenate(split(turned, 3), axis=0)
    gram[...] = jnp.dot(turned, left, precision=exact, preferred_element_type=f32)
    share = gram[pl.ds(pl.multiple_of(line_index() * 8, 8), 8), :]
    empty = jnp.zeros((8, rank), f32)
    even = lax.axis_index("zl") == 0
    padded = jnp.concatenate(
        [jnp.where(even, share, empty), jnp.where(even, empty, share)], axis=1
    )
    for j in range(32):
        out[j, tall:, :] = padded
    for k in range(blocks):
        high, low = split(keep[k] + received[k], 2)
        term = dot(pieces, high) + dot(pieces, low)
        block = term[:rank] + term[rank : 2 * rank] + term[2 * rank :]
        for x in range(4):
            for t in range(5):
                out[8 * x + k, 16 * t : 16 * (t + 1), :] = block[
                    16 * x : 16 * (x + 1), 128 * t : 128 * (t + 1)
                ]


def right_factor(mine, theirs, keep, received):
    return call(
        right_kernel, "right", 16, 10_000_000,
        in_specs=[vmem] * 4,
        out_specs=[vmem, vmem],
        out_shape=[shape(32, tall + 8, 128), shape(rows, rank)],
        scratch_shapes=[pltpu.VMEM((rank, rank), f32)],
    )(mine, theirs, keep, received)


def plane_sum_kernel(chunks, out):
    total = chunks[0]
    for j in range(1, 32):
        total += chunks[j]
    for z in range(4):
        out[z] = total


def plane_sum(chunks):
    return call(
        plane_sum_kernel, "plane_sum", 8, 3_000_000,
        in_specs=[vmem],
        out_specs=vmem,
        out_shape=shape(4, tall + 8, 128),
    )(chunks)


def line_sum_kernel(chunks, out, gram):
    total = chunks[0, :tall, :]
    for j in range(1, 4):
        total += chunks[j, :tall, :]
    for j in range(32):
        out[j] = total
    for j in range(4):
        pair = chunks[j, tall:, :]
        gram[16 * j : 16 * j + 8, :] = pair
        gram[16 * j + 8 : 16 * (j + 1), :] = jnp.concatenate(
            [pair[:, rank:], pair[:, :rank]], axis=1
        )


def line_sum(chunks):
    return call(
        line_sum_kernel, "line_sum", 8, 3_000_000,
        in_specs=[vmem],
        out_specs=[vmem, vmem],
        out_shape=[shape(32, tall, 128), shape(rank, 2 * rank)],
    )(chunks)


def inverse(gram):
    size = (rank, 2 * rank)
    row = lax.broadcasted_iota(jnp.int32, size, 0)
    lane = lax.broadcasted_iota(jnp.int32, size, 1)
    work = jnp.where(lane < rank, gram, (lane == row + rank).astype(f32))
    step = 8
    for k in range(0, rank, step):
        columns = [jnp.broadcast_to(work[:, k + j : k + j + 1], size) for j in range(step)]
        block = [[columns[j][k + i : k + i + 1, :] for j in range(step)] for i in range(step)]
        pivots = [work[k + i : k + i + 1, :] for i in range(step)]
        for j in range(step):
            scale = 1.0 / block[j][j]
            pivots[j] = pivots[j] * scale
            for m in range(j + 1, step):
                block[j][m] = block[j][m] * scale
            for i in range(step):
                if i != j:
                    pivots[i] = pivots[i] - block[i][j] * pivots[j]
                    for m in range(j + 1, step):
                        block[i][m] = block[i][m] - block[i][j] * block[j][m]
        for j in range(step):
            work = work - columns[j] * pivots[j]
        for j in range(step):
            work = jnp.where(row == k + j, pivots[j], work)
    return work[:, rank:]


def solve(gram, left):
    solved = jnp.dot(
        left, inverse(gram) * (1.0 / groups), precision=exact, preferred_element_type=f32
    )
    high, low = split(solved, 2)
    return jnp.concatenate([high, high, low], axis=1)


def block_copy(k, offset, held, new_error, sems):
    begin = pl.multiple_of((2 * k + offset) * narrow, narrow)
    return pltpu.make_async_copy(held.at[k], new_error.at[:, pl.ds(begin, narrow)], sems.at[k])


def approx_block(k, factor, right):
    tiles = []
    for t in range(5):
        part = pl.ds(16 * t, 16)
        tiles.append(jnp.concatenate([right[8 * x + k, part, :] for x in range(4)], axis=0))
    high, low = split(jnp.concatenate(tiles, axis=1), 2)
    return dot(factor, jnp.concatenate([high, low, high], axis=0))


def own_kernel(
    gram, left, right, merged, weights, momentum, new_error, new_weights, new_momentum, factor,
    held, held_weights, held_momentum, sems, state_sems,
):
    core, z = lax.axis_index("core"), line_index()
    solved = solve(gram[...], left[...])
    factor[...] = solved
    copies = []
    state = [
        pltpu.make_async_copy(held_weights, new_weights, state_sems.at[0]),
        pltpu.make_async_copy(held_momentum, new_momentum, state_sems.at[1]),
    ]
    for k in range(blocks):
        approx = approx_block(k, solved, right)
        held[k] = (merged[k] - approx).astype(bf16)
        copies.append(block_copy(k, core, held, new_error, sems))
        copies[-1].start()

        @pl.when(z == k)
        def _():
            moved = momentum_decay * momentum[...] + approx
            held_momentum[...] = moved
            held_weights[...] = weights[...] - outer_rate * (approx + momentum_decay * moved)

    for copy in state:
        copy.start()
    for copy in copies + state:
        copy.wait()


def finish_own(gram, left, right, merged, weights, momentum):
    return call(
        own_kernel, "own", 16, 16_000_000,
        in_specs=[vmem] * 6,
        out_specs=[hbm, hbm, hbm, vmem],
        out_shape=[
            shape(rows, cols, dtype=bf16),
            shape(rows, narrow),
            shape(rows, narrow),
            shape(rows, 3 * rank, dtype=bf16),
        ],
        scratch_shapes=[
            pltpu.VMEM((blocks, rows, narrow), bf16),
            pltpu.VMEM((rows, narrow), f32),
            pltpu.VMEM((rows, narrow), f32),
            pltpu.SemaphoreType.DMA((blocks,)),
            pltpu.SemaphoreType.DMA((2,)),
        ],
    )(gram, left, right, merged, weights, momentum)


def other_kernel(factor, right, merged, partial, new_error, held, sems):
    offset = 1 - lax.axis_index("core")
    left = factor[...]
    copies = []
    for k in range(blocks):
        held[k] = (merged[k] - approx_block(k, left, right)).astype(bf16)
        copies.append(block_copy(k, offset, held, new_error, sems))
        copies[-1].start()
    for copy in copies:
        copy.wait()


def finish_other(factor, right, merged, partial):
    return call(
        other_kernel, "other", 16, 8_000_000,
        in_specs=[vmem, vmem, vmem, hbm],
        out_specs=hbm,
        out_shape=shape(rows, cols, dtype=bf16),
        input_output_aliases={3: 0},
        scratch_shapes=[
            pltpu.VMEM((blocks, rows, narrow), bf16),
            pltpu.SemaphoreType.DMA((blocks,)),
        ],
    )(factor, right, merged, partial)


def swap(value):
    return lax.ppermute(value, "core", [(0, 1), (1, 0)])


def local(drift, error, start, weights, momentum):
    copies, keep, send = left_factor(drift[0], error[0], start.T)
    received = swap(send)
    mine = lax.all_to_all(copies, ("zh", "zl"), 0, 0)
    chunks, left = right_factor(mine, swap(mine), keep, received)
    plane = plane_sum(lax.all_to_all(chunks, ("x", "y", "zl"), 0, 0))
    line, gram = line_sum(lax.all_to_all(plane, "zh", 0, 0))
    own = lax.all_to_all(line, ("x", "y", "zl"), 0, 0)
    other = swap(own)
    partial, new_weights, new_momentum, factor = finish_own(
        gram, left, own, keep, weights, momentum
    )
    new_error = finish_other(factor, other, send, partial)
    return new_weights, new_error[None], new_momentum


def solution(mesh):
    fine = Mesh(mesh.devices.reshape(4, 2, 2, 4, 4), ("zh", "zl", "core", "x", "y"))
    replica, fsdp = ("zh", "zl", "core"), ("x", "y")
    return jax.shard_map(
        local,
        mesh=fine,
        in_specs=(
            P(replica, fsdp, None),
            P(replica, fsdp, None),
            P(),
            P(fsdp, replica),
            P(fsdp, replica),
        ),
        out_specs=(P(fsdp, replica), P(replica, fsdp, None), P(fsdp, replica)),
        check_vma=False,
    )
```

```python
import jax
import jax.numpy as jnp
from jax import lax
from jax.experimental import pallas as pl
from jax.experimental.pallas import tpu as pltpu
from jax.sharding import Mesh, PartitionSpec as P

outer_rate = 0.7
momentum_decay = 0.9

rows = 160
cols = 10240
rank = 64
narrow = 640
wide = 1280
blocks = 8
groups = 16
tall = 80
reads = 4
chunk = cols // reads
f32 = jnp.float32
bf16 = jnp.bfloat16
exact = lax.Precision.HIGHEST
mib = 1024 * 1024
hbm = pl.BlockSpec(memory_space=pltpu.HBM)
vmem = pl.BlockSpec(memory_space=pltpu.VMEM)


def split(value, pieces):
    out = []
    for _ in range(pieces - 1):
        head = value.astype(bf16)
        out.append(head)
        value = value - head.astype(f32)
    out.append(value.astype(bf16))
    return out


def dot(a, b):
    return jnp.dot(a, b, preferred_element_type=f32)


def dot_rows(a, b):
    return lax.dot_general(a, b, (((1,), (1,)), ((), ())), preferred_element_type=f32)


def call(kernel, name, size, moved, **kwargs):
    return pl.pallas_call(
        kernel,
        name=name,
        compiler_params=pltpu.CompilerParams(vmem_limit_bytes=size * mib),
        cost_estimate=pl.CostEstimate(flops=0, bytes_accessed=moved, transcendentals=0),
        **kwargs,
    )


def shape(*dims, dtype=f32):
    return jax.ShapeDtypeStruct(dims, dtype)


def pack(value):
    count = value.shape[0] // 2
    return jnp.concatenate([value[:count], value[count:]], axis=1)


def unpack(value):
    return jnp.concatenate([value[:, :rank], value[:, rank:]], axis=0)


def left_kernel(drift, error, start, mine, theirs, keep, send, drifts, errors, starts, acc, sems):
    first = lax.axis_index("core") == 0
    copies = []
    for i in range(reads):
        lanes = pl.ds(i * chunk, chunk)
        group = [
            pltpu.make_async_copy(start.at[:, lanes], starts.at[i], sems.at[i, 0]),
            pltpu.make_async_copy(drift.at[:, lanes], drifts.at[i], sems.at[i, 1]),
            pltpu.make_async_copy(error.at[:, lanes], errors.at[i], sems.at[i, 2]),
        ]
        for copy in group:
            copy.start()
        copies.append(group)
    for i in range(reads):
        for copy in copies[i]:
            copy.wait()
        both = jnp.concatenate([drifts[i], errors[i]], axis=0)
        term = dot_rows(both, jnp.concatenate(split(starts[i], 2), axis=0))
        if i == 0:
            acc[...] = term
        else:
            acc[...] += term
        merged = drifts[i].astype(f32) + errors[i].astype(f32)
        for j in range(chunk // wide):
            even = merged[:, wide * j : wide * j + narrow]
            odd = merged[:, wide * j + narrow : wide * (j + 1)]
            k = i * (chunk // wide) + j
            keep[k] = jnp.where(first, even, odd)
            send[k] = jnp.where(first, odd, even)
    total = acc[:rows, :] + acc[rows:, :]
    left = total[:, :rank] + total[:, rank:]
    upper, lower = pack(left[: rows // 2]), pack(left[rows // 2 :])
    mine[...] = jnp.where(first, upper, lower)
    theirs[...] = jnp.where(first, lower, upper)


def left_factor(drift, error, start):
    inputs = [pltpu.with_memory_space_constraint(v, pltpu.HBM) for v in (drift, error, start)]
    return call(
        left_kernel, "left", 24, 13_000_000,
        in_specs=[hbm, hbm, hbm],
        out_specs=[vmem] * 4,
        out_shape=[
            pltpu.VMEM((rows // 4, 2 * rank), f32),
            pltpu.VMEM((rows // 4, 2 * rank), f32),
            pltpu.VMEM((blocks, rows, narrow), f32),
            pltpu.VMEM((blocks, rows, narrow), f32),
        ],
        scratch_shapes=[
            pltpu.VMEM((reads, rows, chunk), bf16),
            pltpu.VMEM((reads, rows, chunk), bf16),
            pltpu.VMEM((reads, rank, chunk), f32),
            pltpu.VMEM((2 * rows, 2 * rank), f32),
            pltpu.SemaphoreType.DMA((reads, 3)),
        ],
    )(*inputs)


def pair_sum_kernel(mine, received, out):
    total = mine[...] + received[...]
    for z in range(8):
        out[z] = total


def pair_sum(mine, received):
    return call(
        pair_sum_kernel, "pair_sum", 4, 500_000,
        in_specs=[vmem, vmem],
        out_specs=vmem,
        out_shape=shape(8, rows // 4, 2 * rank),
    )(mine, received)


def line_index():
    return 2 * lax.axis_index("zh") + lax.axis_index("zl")


def right_kernel(mine, theirs, keep, received, out, left_out, gram):
    own = unpack(jnp.sum(mine[...], axis=0)) * (1.0 / groups)
    other = unpack(jnp.sum(theirs[...], axis=0)) * (1.0 / groups)
    first = lax.axis_index("core") == 0
    left = jnp.concatenate([jnp.where(first, own, other), jnp.where(first, other, own)], axis=0)
    left_out[...] = left
    turned = left.T
    pieces = jnp.concatenate(split(turned, 3), axis=0)
    gram[...] = jnp.dot(turned, left, precision=exact, preferred_element_type=f32)
    share = gram[pl.ds(pl.multiple_of(line_index() * 8, 8), 8), :]
    empty = jnp.zeros((8, rank), f32)
    even = lax.axis_index("zl") == 0
    padded = jnp.concatenate(
        [jnp.where(even, share, empty), jnp.where(even, empty, share)], axis=1
    )
    for j in range(32):
        out[j, tall:, :] = padded
    for k in range(blocks):
        high, low = split(keep[k] + received[k], 2)
        term = dot(pieces, high) + dot(pieces, low)
        block = term[:rank] + term[rank : 2 * rank] + term[2 * rank :]
        for x in range(4):
            for t in range(5):
                out[8 * x + k, 16 * t : 16 * (t + 1), :] = block[
                    16 * x : 16 * (x + 1), 128 * t : 128 * (t + 1)
                ]


def right_factor(mine, theirs, keep, received):
    return call(
        right_kernel, "right", 16, 10_000_000,
        in_specs=[vmem] * 4,
        out_specs=[vmem, vmem],
        out_shape=[shape(32, tall + 8, 128), shape(rows, rank)],
        scratch_shapes=[pltpu.VMEM((rank, rank), f32)],
    )(mine, theirs, keep, received)


def plane_sum_kernel(chunks, out):
    total = chunks[0]
    for j in range(1, 32):
        total += chunks[j]
    for z in range(4):
        out[z] = total


def plane_sum(chunks):
    return call(
        plane_sum_kernel, "plane_sum", 8, 3_000_000,
        in_specs=[vmem],
        out_specs=vmem,
        out_shape=shape(4, tall + 8, 128),
    )(chunks)


def line_sum_kernel(chunks, out, gram):
    total = chunks[0, :tall, :]
    for j in range(1, 4):
        total += chunks[j, :tall, :]
    for j in range(32):
        out[j] = total
    for j in range(4):
        pair = chunks[j, tall:, :]
        gram[16 * j : 16 * j + 8, :] = pair
        gram[16 * j + 8 : 16 * (j + 1), :] = jnp.concatenate(
            [pair[:, rank:], pair[:, :rank]], axis=1
        )


def line_sum(chunks):
    return call(
        line_sum_kernel, "line_sum", 8, 3_000_000,
        in_specs=[vmem],
        out_specs=[vmem, vmem],
        out_shape=[shape(32, tall, 128), shape(rank, 2 * rank)],
    )(chunks)


def inverse(gram):
    size = (rank, 2 * rank)
    row = lax.broadcasted_iota(jnp.int32, size, 0)
    lane = lax.broadcasted_iota(jnp.int32, size, 1)
    work = jnp.where(lane < rank, gram, (lane == row + rank).astype(f32))
    step = 8
    for k in range(0, rank, step):
        columns = [jnp.broadcast_to(work[:, k + j : k + j + 1], size) for j in range(step)]
        block = [[columns[j][k + i : k + i + 1, :] for j in range(step)] for i in range(step)]
        pivots = [work[k + i : k + i + 1, :] for i in range(step)]
        for j in range(step):
            scale = 1.0 / block[j][j]
            pivots[j] = pivots[j] * scale
            for m in range(j + 1, step):
                block[j][m] = block[j][m] * scale
            for i in range(step):
                if i != j:
                    pivots[i] = pivots[i] - block[i][j] * pivots[j]
                    for m in range(j + 1, step):
                        block[i][m] = block[i][m] - block[i][j] * block[j][m]
        for j in range(step):
            work = work - columns[j] * pivots[j]
        for j in range(step):
            work = jnp.where(row == k + j, pivots[j], work)
    return work[:, rank:]


def solve(gram, left):
    solved = jnp.dot(
        left, inverse(gram) * (1.0 / groups), precision=exact, preferred_element_type=f32
    )
    high, low = split(solved, 2)
    return jnp.concatenate([high, high, low], axis=1)


def block_copy(k, offset, held, new_error, sems):
    begin = pl.multiple_of((2 * k + offset) * narrow, narrow)
    return pltpu.make_async_copy(held.at[k], new_error.at[:, pl.ds(begin, narrow)], sems.at[k])


def approx_block(k, factor, right):
    tiles = []
    for t in range(5):
        part = pl.ds(16 * t, 16)
        tiles.append(jnp.concatenate([right[8 * x + k, part, :] for x in range(4)], axis=0))
    high, low = split(jnp.concatenate(tiles, axis=1), 2)
    return dot(factor, jnp.concatenate([high, low, high], axis=0))


def own_kernel(
    gram, left, right, merged, weights, momentum, new_error, new_weights, new_momentum, factor,
    held, held_weights, held_momentum, sems, state_sems,
):
    core, z = lax.axis_index("core"), line_index()
    solved = solve(gram[...], left[...])
    factor[...] = solved
    copies = []
    state = [
        pltpu.make_async_copy(held_weights, new_weights, state_sems.at[0]),
        pltpu.make_async_copy(held_momentum, new_momentum, state_sems.at[1]),
    ]
    for k in range(blocks):
        approx = approx_block(k, solved, right)
        held[k] = (merged[k] - approx).astype(bf16)
        copies.append(block_copy(k, core, held, new_error, sems))
        copies[-1].start()

        @pl.when(z == k)
        def _():
            moved = momentum_decay * momentum[...] + approx
            held_momentum[...] = moved
            held_weights[...] = weights[...] - outer_rate * (approx + momentum_decay * moved)

    for copy in state:
        copy.start()
    for copy in copies + state:
        copy.wait()


def finish_own(gram, left, right, merged, weights, momentum):
    return call(
        own_kernel, "own", 16, 16_000_000,
        in_specs=[vmem] * 6,
        out_specs=[hbm, hbm, hbm, vmem],
        out_shape=[
            shape(rows, cols, dtype=bf16),
            shape(rows, narrow),
            shape(rows, narrow),
            shape(rows, 3 * rank, dtype=bf16),
        ],
        scratch_shapes=[
            pltpu.VMEM((blocks, rows, narrow), bf16),
            pltpu.VMEM((rows, narrow), f32),
            pltpu.VMEM((rows, narrow), f32),
            pltpu.SemaphoreType.DMA((blocks,)),
            pltpu.SemaphoreType.DMA((2,)),
        ],
    )(gram, left, right, merged, weights, momentum)


def other_kernel(factor, right, merged, partial, new_error, held, sems):
    offset = 1 - lax.axis_index("core")
    left = factor[...]
    copies = []
    for k in range(blocks):
        held[k] = (merged[k] - approx_block(k, left, right)).astype(bf16)
        copies.append(block_copy(k, offset, held, new_error, sems))
        copies[-1].start()
    for copy in copies:
        copy.wait()


def finish_other(factor, right, merged, partial):
    return call(
        other_kernel, "other", 16, 8_000_000,
        in_specs=[vmem, vmem, vmem, hbm],
        out_specs=hbm,
        out_shape=shape(rows, cols, dtype=bf16),
        input_output_aliases={3: 0},
        scratch_shapes=[
            pltpu.VMEM((blocks, rows, narrow), bf16),
            pltpu.SemaphoreType.DMA((blocks,)),
        ],
    )(factor, right, merged, partial)


def swap(value):
    return lax.ppermute(value, "core", [(0, 1), (1, 0)])


def local(drift, error, start, weights, momentum):
    mine, theirs, keep, send = left_factor(drift[0], error[0], start.T)
    theirs, send = lax.optimization_barrier((swap(theirs), send))
    received = swap(send)
    mine = lax.all_to_all(pair_sum(mine, theirs), ("zh", "zl"), 0, 0)
    chunks, left = right_factor(mine, swap(mine), keep, received)
    plane = plane_sum(lax.all_to_all(chunks, ("x", "y", "zl"), 0, 0))
    line, gram = line_sum(lax.all_to_all(plane, "zh", 0, 0))
    own = lax.all_to_all(line, ("x", "y", "zl"), 0, 0)
    other = swap(own)
    partial, new_weights, new_momentum, factor = finish_own(
        gram, left, own, keep, weights, momentum
    )
    new_error = finish_other(factor, other, send, partial)
    return new_weights, new_error[None], new_momentum


def solution(mesh):
    fine = Mesh(mesh.devices.reshape(4, 2, 2, 4, 4), ("zh", "zl", "core", "x", "y"))
    replica, fsdp = ("zh", "zl", "core"), ("x", "y")
    return jax.shard_map(
        local,
        mesh=fine,
        in_specs=(
            P(replica, fsdp, None),
            P(replica, fsdp, None),
            P(),
            P(fsdp, replica),
            P(fsdp, replica),
        ),
        out_specs=(P(fsdp, replica), P(replica, fsdp, None), P(fsdp, replica)),
        check_vma=False,
    )
```

```python
import jax
import jax.numpy as jnp
from jax import lax
from jax.experimental import pallas as pl
from jax.experimental.pallas import tpu as pltpu
from jax.sharding import Mesh, PartitionSpec as P

outer_rate = 0.7
momentum_decay = 0.9

rows = 160
cols = 10240
rank = 64
narrow = 640
wide = 1280
blocks = 8
groups = 16
tall = 80
reads = 4
chunk = cols // reads
f32 = jnp.float32
bf16 = jnp.bfloat16
exact = lax.Precision.HIGHEST
mib = 1024 * 1024
hbm = pl.BlockSpec(memory_space=pltpu.HBM)
vmem = pl.BlockSpec(memory_space=pltpu.VMEM)


def split(value, pieces):
    out = []
    for _ in range(pieces - 1):
        head = value.astype(bf16)
        out.append(head)
        value = value - head.astype(f32)
    out.append(value.astype(bf16))
    return out


def dot(a, b):
    return jnp.dot(a, b, preferred_element_type=f32)


def dot_rows(a, b):
    return lax.dot_general(a, b, (((1,), (1,)), ((), ())), preferred_element_type=f32)


def call(kernel, name, size, moved, **kwargs):
    return pl.pallas_call(
        kernel,
        name=name,
        compiler_params=pltpu.CompilerParams(vmem_limit_bytes=size * mib),
        cost_estimate=pl.CostEstimate(flops=0, bytes_accessed=moved, transcendentals=0),
        **kwargs,
    )


def shape(*dims, dtype=f32):
    return jax.ShapeDtypeStruct(dims, dtype)


def pack(value):
    count = value.shape[0] // 2
    return jnp.concatenate([value[:count], value[count:]], axis=1)


def unpack(value):
    return jnp.concatenate([value[:, :rank], value[:, rank:]], axis=0)


def left_kernel(drift, error, start, mine, theirs, keep, send, drifts, errors, starts, acc, sems):
    first = lax.axis_index("core") == 0

    def copies(i):
        lanes = pl.ds(pl.multiple_of(i * chunk, chunk), chunk)
        return [
            pltpu.make_async_copy(start.at[:, lanes], starts.at[i], sems.at[i, 0]),
            pltpu.make_async_copy(drift.at[:, lanes], drifts.at[i], sems.at[i, 1]),
            pltpu.make_async_copy(error.at[:, lanes], errors.at[i], sems.at[i, 2]),
        ]

    for i in range(reads):
        for copy in copies(i):
            copy.start()
    acc[...] = jnp.zeros_like(acc)

    @pl.loop(0, reads)
    def _(i):
        for copy in copies(i):
            copy.wait()
        first_part, second_part = drifts[i], errors[i]
        merged = first_part.astype(f32) + second_part.astype(f32)
        both = jnp.concatenate([first_part, second_part], axis=0)
        acc[...] += dot_rows(both, jnp.concatenate(split(starts[i], 2), axis=0))
        for j in range(chunk // wide):
            even = merged[:, wide * j : wide * j + narrow]
            odd = merged[:, wide * j + narrow : wide * (j + 1)]
            k = i * (chunk // wide) + j
            keep[k] = jnp.where(first, even, odd)
            send[k] = jnp.where(first, odd, even)
    total = acc[:rows, :] + acc[rows:, :]
    left = total[:, :rank] + total[:, rank:]
    upper, lower = pack(left[: rows // 2]), pack(left[rows // 2 :])
    mine[...] = jnp.where(first, upper, lower)
    theirs[...] = jnp.where(first, lower, upper)


def left_factor(drift, error, start):
    inputs = [pltpu.with_memory_space_constraint(v, pltpu.HBM) for v in (drift, error, start)]
    return call(
        left_kernel, "left", 24, 13_000_000,
        in_specs=[hbm, hbm, hbm],
        out_specs=[vmem] * 4,
        out_shape=[
            pltpu.VMEM((rows // 4, 2 * rank), f32),
            pltpu.VMEM((rows // 4, 2 * rank), f32),
            pltpu.VMEM((blocks, rows, narrow), f32),
            pltpu.VMEM((blocks, rows, narrow), f32),
        ],
        scratch_shapes=[
            pltpu.VMEM((reads, rows, chunk), bf16),
            pltpu.VMEM((reads, rows, chunk), bf16),
            pltpu.VMEM((reads, rank, chunk), f32),
            pltpu.VMEM((2 * rows, 2 * rank), f32),
            pltpu.SemaphoreType.DMA((reads, 3)),
        ],
    )(*inputs)


def pair_sum_kernel(mine, received, out):
    total = mine[...] + received[...]
    for z in range(8):
        out[z] = total


def pair_sum(mine, received):
    return call(
        pair_sum_kernel, "pair_sum", 4, 500_000,
        in_specs=[vmem, vmem],
        out_specs=vmem,
        out_shape=shape(8, rows // 4, 2 * rank),
    )(mine, received)


def line_index():
    return 2 * lax.axis_index("zh") + lax.axis_index("zl")


def right_kernel(mine, theirs, keep, received, out, left_out, gram):
    own = unpack(jnp.sum(mine[...], axis=0)) * (1.0 / groups)
    other = unpack(jnp.sum(theirs[...], axis=0)) * (1.0 / groups)
    first = lax.axis_index("core") == 0
    left = jnp.concatenate([jnp.where(first, own, other), jnp.where(first, other, own)], axis=0)
    left_out[...] = left
    turned = left.T
    pieces = jnp.concatenate(split(turned, 3), axis=0)
    gram[...] = jnp.dot(turned, left, precision=exact, preferred_element_type=f32)
    share = gram[pl.ds(pl.multiple_of(line_index() * 8, 8), 8), :]
    empty = jnp.zeros((8, rank), f32)
    even = lax.axis_index("zl") == 0
    padded = jnp.concatenate(
        [jnp.where(even, share, empty), jnp.where(even, empty, share)], axis=1
    )
    for j in range(32):
        out[j, tall:, :] = padded

    for k in range(blocks):
        high, low = split(keep[k] + received[k], 2)
        term = dot(pieces, high) + dot(pieces, low)
        block = term[:rank] + term[rank : 2 * rank] + term[2 * rank :]
        for x in range(4):
            for t in range(5):
                out[8 * x + k, 16 * t : 16 * (t + 1), :] = block[
                    16 * x : 16 * (x + 1), 128 * t : 128 * (t + 1)
                ]


def right_factor(mine, theirs, keep, received):
    return call(
        right_kernel, "right", 16, 10_000_000,
        in_specs=[vmem] * 4,
        out_specs=[vmem, vmem],
        out_shape=[shape(32, tall + 8, 128), shape(rows, rank)],
        scratch_shapes=[pltpu.VMEM((rank, rank), f32)],
    )(mine, theirs, keep, received)


def plane_sum_kernel(chunks, out):
    total = chunks[0]
    for j in range(1, 32):
        total += chunks[j]
    for z in range(4):
        out[z] = total


def plane_sum(chunks):
    return call(
        plane_sum_kernel, "plane_sum", 8, 3_000_000,
        in_specs=[vmem],
        out_specs=vmem,
        out_shape=shape(4, tall + 8, 128),
    )(chunks)


def line_sum_kernel(chunks, out, gram):
    total = chunks[0, :tall, :]
    for j in range(1, 4):
        total += chunks[j, :tall, :]
    for j in range(32):
        out[j] = total
    for j in range(4):
        pair = chunks[j, tall:, :]
        gram[16 * j : 16 * j + 8, :] = pair
        gram[16 * j + 8 : 16 * (j + 1), :] = jnp.concatenate(
            [pair[:, rank:], pair[:, :rank]], axis=1
        )


def line_sum(chunks):
    return call(
        line_sum_kernel, "line_sum", 8, 3_000_000,
        in_specs=[vmem],
        out_specs=[vmem, vmem],
        out_shape=[shape(32, tall, 128), shape(rank, 2 * rank)],
    )(chunks)


def inverse(gram):
    size = (rank, 2 * rank)
    row = lax.broadcasted_iota(jnp.int32, size, 0)
    lane = lax.broadcasted_iota(jnp.int32, size, 1)
    work = jnp.where(lane < rank, gram, (lane == row + rank).astype(f32))
    step = 8
    count = rank // step

    def eliminate(_, work):
        columns = [
            [jnp.broadcast_to(part[:, j : j + 1], (step, 2 * rank)) for j in range(step)]
            for part in work
        ]
        block = [[columns[0][j][i : i + 1, :] for j in range(step)] for i in range(step)]
        pivots = [work[0][i : i + 1, :] for i in range(step)]
        for j in range(step):
            scale = 1.0 / block[j][j]
            pivots[j] = pivots[j] * scale
            for m in range(j + 1, step):
                block[j][m] = block[j][m] * scale
            for i in range(step):
                if i != j:
                    pivots[i] = pivots[i] - block[i][j] * pivots[j]
                    for m in range(j + 1, step):
                        block[i][m] = block[i][m] - block[i][j] * block[j][m]
        done = []
        for part, factors in zip(work[1:], columns[1:]):
            for j in range(step):
                part = part - factors[j] * pivots[j]
            done.append(part)
        done.append(jnp.concatenate(pivots, axis=0))
        return tuple(pltpu.roll(part, 2 * rank - step, axis=1) for part in done)

    parts = tuple(work[step * i : step * (i + 1)] for i in range(count))
    parts = lax.fori_loop(0, count, eliminate, parts)
    return jnp.concatenate(parts, axis=0)[:, :rank]


def solve(gram, left):
    solved = jnp.dot(
        left, inverse(gram) * (1.0 / groups), precision=exact, preferred_element_type=f32
    )
    high, low = split(solved, 2)
    return jnp.concatenate([high, high, low], axis=1)


def block_copy(k, offset, held, new_error, sems):
    begin = pl.multiple_of((2 * k + offset) * narrow, narrow)
    return pltpu.make_async_copy(held.at[k], new_error.at[:, pl.ds(begin, narrow)], sems.at[k])


def approx_block(k, factor, right):
    tiles = []
    for t in range(5):
        part = pl.ds(16 * t, 16)
        tiles.append(jnp.concatenate([right[8 * x + k, part, :] for x in range(4)], axis=0))
    high, low = split(jnp.concatenate(tiles, axis=1), 2)
    return dot(factor, jnp.concatenate([high, low, high], axis=0))


def own_kernel(
    gram, left, right, merged, weights, momentum, new_error, new_weights, new_momentum, factor,
    held, held_weights, held_momentum, sems, state_sems,
):
    core, z = lax.axis_index("core"), line_index()
    factor[...] = solve(gram[...], left[...])

    @pl.loop(0, blocks)
    def _(k):
        approx = approx_block(k, factor[...], right)
        held[k] = (merged[k] - approx).astype(bf16)
        block_copy(k, core, held, new_error, sems).start()

        @pl.when(z == k)
        def _():
            moved = momentum_decay * momentum[...] + approx
            held_momentum[...] = moved
            held_weights[...] = weights[...] - outer_rate * (approx + momentum_decay * moved)

    state = [
        pltpu.make_async_copy(held_weights, new_weights, state_sems.at[0]),
        pltpu.make_async_copy(held_momentum, new_momentum, state_sems.at[1]),
    ]
    for copy in state:
        copy.start()

    @pl.loop(0, blocks)
    def _(k):
        block_copy(k, core, held, new_error, sems).wait()

    for copy in state:
        copy.wait()


def finish_own(gram, left, right, merged, weights, momentum):
    return call(
        own_kernel, "own", 16, 16_000_000,
        in_specs=[vmem] * 6,
        out_specs=[hbm, hbm, hbm, vmem],
        out_shape=[
            shape(rows, cols, dtype=bf16),
            shape(rows, narrow),
            shape(rows, narrow),
            shape(rows, 3 * rank, dtype=bf16),
        ],
        scratch_shapes=[
            pltpu.VMEM((blocks, rows, narrow), bf16),
            pltpu.VMEM((rows, narrow), f32),
            pltpu.VMEM((rows, narrow), f32),
            pltpu.SemaphoreType.DMA((blocks,)),
            pltpu.SemaphoreType.DMA((2,)),
        ],
    )(gram, left, right, merged, weights, momentum)


def other_kernel(factor, right, merged, partial, new_error, held, sems):
    offset = 1 - lax.axis_index("core")

    for k in range(blocks):
        held[k] = (merged[k] - approx_block(k, factor[...], right)).astype(bf16)
        block_copy(k, offset, held, new_error, sems).start()

    @pl.loop(0, blocks)
    def _(k):
        block_copy(k, offset, held, new_error, sems).wait()


def finish_other(factor, right, merged, partial):
    return call(
        other_kernel, "other", 16, 8_000_000,
        in_specs=[vmem, vmem, vmem, hbm],
        out_specs=hbm,
        out_shape=shape(rows, cols, dtype=bf16),
        input_output_aliases={3: 0},
        scratch_shapes=[
            pltpu.VMEM((blocks, rows, narrow), bf16),
            pltpu.SemaphoreType.DMA((blocks,)),
        ],
    )(factor, right, merged, partial)


def swap(value):
    return lax.ppermute(value, "core", [(0, 1), (1, 0)])


def local(drift, error, start, weights, momentum):
    mine, theirs, keep, send = left_factor(drift[0], error[0], start.T)
    theirs, send = lax.optimization_barrier((swap(theirs), send))
    received = swap(send)
    mine = lax.all_to_all(pair_sum(mine, theirs), ("zh", "zl"), 0, 0)
    chunks, left = right_factor(mine, swap(mine), keep, received)
    plane = plane_sum(lax.all_to_all(chunks, ("x", "y", "zl"), 0, 0))
    line, gram = line_sum(lax.all_to_all(plane, "zh", 0, 0))
    own = lax.all_to_all(line, ("x", "y", "zl"), 0, 0)
    other = swap(own)
    partial, new_weights, new_momentum, factor = finish_own(
        gram, left, own, keep, weights, momentum
    )
    new_error = finish_other(factor, other, send, partial)
    return new_weights, new_error[None], new_momentum


def solution(mesh):
    fine = Mesh(mesh.devices.reshape(4, 2, 2, 4, 4), ("zh", "zl", "core", "x", "y"))
    replica, fsdp = ("zh", "zl", "core"), ("x", "y")
    return jax.shard_map(
        local,
        mesh=fine,
        in_specs=(
            P(replica, fsdp, None),
            P(replica, fsdp, None),
            P(),
            P(fsdp, replica),
            P(fsdp, replica),
        ),
        out_specs=(P(fsdp, replica), P(replica, fsdp, None), P(fsdp, replica)),
        check_vma=False,
    )
```

```python
import jax
import jax.numpy as jnp
from jax import lax
from jax.experimental import pallas as pl
from jax.experimental.pallas import tpu as pltpu
from jax.sharding import Mesh, PartitionSpec as P

outer_rate = 0.7
momentum_decay = 0.9

rows = 160
cols = 10240
rank = 64
narrow = 640
wide = 1280
blocks = 8
groups = 16
tall = 80
reads = 4
chunk = cols // reads
f32 = jnp.float32
bf16 = jnp.bfloat16
exact = lax.Precision.HIGHEST
mib = 1024 * 1024
hbm = pl.BlockSpec(memory_space=pltpu.HBM)
vmem = pl.BlockSpec(memory_space=pltpu.VMEM)


def split(value, pieces):
    out = []
    for _ in range(pieces - 1):
        head = value.astype(bf16)
        out.append(head)
        value = value - head.astype(f32)
    out.append(value.astype(bf16))
    return out


def dot(a, b):
    return jnp.dot(a, b, preferred_element_type=f32)


def dot_rows(a, b):
    return lax.dot_general(a, b, (((1,), (1,)), ((), ())), preferred_element_type=f32)


def call(kernel, name, size, moved, **kwargs):
    return pl.pallas_call(
        kernel,
        name=name,
        compiler_params=pltpu.CompilerParams(vmem_limit_bytes=size * mib),
        cost_estimate=pl.CostEstimate(flops=0, bytes_accessed=moved, transcendentals=0),
        **kwargs,
    )


def shape(*dims, dtype=f32):
    return jax.ShapeDtypeStruct(dims, dtype)


def pack(value):
    count = value.shape[0] // 2
    return jnp.concatenate([value[:count], value[count:]], axis=1)


def unpack(value):
    return jnp.concatenate([value[:, :rank], value[:, rank:]], axis=0)


def left_kernel(drift, error, start, mine, theirs, keep, send, drifts, errors, starts, acc, sems):
    first = lax.axis_index("core") == 0

    def copies(i):
        lanes = pl.ds(pl.multiple_of(i * chunk, chunk), chunk)
        return [
            pltpu.make_async_copy(start.at[:, lanes], starts.at[i], sems.at[i, 0]),
            pltpu.make_async_copy(drift.at[:, lanes], drifts.at[i], sems.at[i, 1]),
            pltpu.make_async_copy(error.at[:, lanes], errors.at[i], sems.at[i, 2]),
        ]

    for i in range(reads):
        for copy in copies(i):
            copy.start()
    acc[...] = jnp.zeros_like(acc)

    @pl.loop(0, reads)
    def _(i):
        for copy in copies(i):
            copy.wait()
        first_part, second_part = drifts[i], errors[i]
        merged = first_part.astype(f32) + second_part.astype(f32)
        both = jnp.concatenate([first_part, second_part], axis=0)
        acc[...] += dot_rows(both, jnp.concatenate(split(starts[i], 2), axis=0))
        for j in range(chunk // wide):
            even = merged[:, wide * j : wide * j + narrow]
            odd = merged[:, wide * j + narrow : wide * (j + 1)]
            k = i * (chunk // wide) + j
            keep[k] = jnp.where(first, even, odd)
            send[k] = jnp.where(first, odd, even)
    total = acc[:rows, :] + acc[rows:, :]
    left = total[:, :rank] + total[:, rank:]
    upper, lower = pack(left[: rows // 2]), pack(left[rows // 2 :])
    mine[...] = jnp.where(first, upper, lower)
    theirs[...] = jnp.where(first, lower, upper)


def left_factor(drift, error, start):
    inputs = [pltpu.with_memory_space_constraint(v, pltpu.HBM) for v in (drift, error, start)]
    return call(
        left_kernel, "left", 24, 13_000_000,
        in_specs=[hbm, hbm, hbm],
        out_specs=[vmem] * 4,
        out_shape=[
            pltpu.VMEM((rows // 4, 2 * rank), f32),
            pltpu.VMEM((rows // 4, 2 * rank), f32),
            pltpu.VMEM((blocks, rows, narrow), f32),
            pltpu.VMEM((blocks, rows, narrow), f32),
        ],
        scratch_shapes=[
            pltpu.VMEM((reads, rows, chunk), bf16),
            pltpu.VMEM((reads, rows, chunk), bf16),
            pltpu.VMEM((reads, rank, chunk), f32),
            pltpu.VMEM((2 * rows, 2 * rank), f32),
            pltpu.SemaphoreType.DMA((reads, 3)),
        ],
    )(*inputs)


def pair_sum_kernel(mine, received, out):
    total = mine[...] + received[...]
    for z in range(8):
        out[z] = total


def pair_sum(mine, received):
    return call(
        pair_sum_kernel, "pair_sum", 4, 500_000,
        in_specs=[vmem, vmem],
        out_specs=vmem,
        out_shape=shape(8, rows // 4, 2 * rank),
    )(mine, received)


def line_index():
    return 2 * lax.axis_index("zh") + lax.axis_index("zl")


def right_kernel(mine, theirs, keep, received, out, left_out, gram):
    own = unpack(jnp.sum(mine[...], axis=0)) * (1.0 / groups)
    other = unpack(jnp.sum(theirs[...], axis=0)) * (1.0 / groups)
    first = lax.axis_index("core") == 0
    left = jnp.concatenate([jnp.where(first, own, other), jnp.where(first, other, own)], axis=0)
    left_out[...] = left
    turned = left.T
    pieces = jnp.concatenate(split(turned, 3), axis=0)
    gram[...] = jnp.dot(turned, left, precision=exact, preferred_element_type=f32)
    share = gram[pl.ds(pl.multiple_of(line_index() * 8, 8), 8), :]
    empty = jnp.zeros((8, rank), f32)
    even = lax.axis_index("zl") == 0
    padded = jnp.concatenate(
        [jnp.where(even, share, empty), jnp.where(even, empty, share)], axis=1
    )
    for j in range(32):
        out[j, tall:, :] = padded

    for k in range(blocks):
        high, low = split(keep[k] + received[k], 2)
        term = dot(pieces, high) + dot(pieces, low)
        block = term[:rank] + term[rank : 2 * rank] + term[2 * rank :]
        for x in range(4):
            for t in range(5):
                out[8 * x + k, 16 * t : 16 * (t + 1), :] = block[
                    16 * x : 16 * (x + 1), 128 * t : 128 * (t + 1)
                ]


def right_factor(mine, theirs, keep, received):
    return call(
        right_kernel, "right", 16, 10_000_000,
        in_specs=[vmem] * 4,
        out_specs=[vmem, vmem],
        out_shape=[shape(32, tall + 8, 128), shape(rows, rank)],
        scratch_shapes=[pltpu.VMEM((rank, rank), f32)],
    )(mine, theirs, keep, received)


def plane_sum_kernel(chunks, out):
    total = chunks[0]
    for j in range(1, 32):
        total += chunks[j]
    for z in range(4):
        out[z] = total


def plane_sum(chunks):
    return call(
        plane_sum_kernel, "plane_sum", 8, 3_000_000,
        in_specs=[vmem],
        out_specs=vmem,
        out_shape=shape(4, tall + 8, 128),
    )(chunks)


def line_sum_kernel(chunks, out, gram):
    total = chunks[0, :tall, :]
    for j in range(1, 4):
        total += chunks[j, :tall, :]
    for j in range(32):
        out[j] = total
    for j in range(4):
        pair = chunks[j, tall:, :]
        gram[16 * j : 16 * j + 8, :] = pair
        gram[16 * j + 8 : 16 * (j + 1), :] = jnp.concatenate(
            [pair[:, rank:], pair[:, :rank]], axis=1
        )


def line_sum(chunks):
    return call(
        line_sum_kernel, "line_sum", 8, 3_000_000,
        in_specs=[vmem],
        out_specs=[vmem, vmem],
        out_shape=[shape(32, tall, 128), shape(rank, 2 * rank)],
    )(chunks)


def inverse(gram):
    size = (rank, 2 * rank)
    row = lax.broadcasted_iota(jnp.int32, size, 0)
    lane = lax.broadcasted_iota(jnp.int32, size, 1)
    work = jnp.where(lane < rank, gram, (lane == row + rank).astype(f32))
    step = 8
    count = rank // step

    def eliminate(_, work):
        columns = [
            [jnp.broadcast_to(part[:, j : j + 1], (step, 2 * rank)) for j in range(step)]
            for part in work
        ]
        block = [[columns[0][j][i : i + 1, :] for j in range(step)] for i in range(step)]
        pivots = [work[0][i : i + 1, :] for i in range(step)]
        for j in range(step):
            scale = 1.0 / block[j][j]
            pivots[j] = pivots[j] * scale
            for m in range(j + 1, step):
                block[j][m] = block[j][m] * scale
            for i in range(step):
                if i != j:
                    pivots[i] = pivots[i] - block[i][j] * pivots[j]
                    for m in range(j + 1, step):
                        block[i][m] = block[i][m] - block[i][j] * block[j][m]
        done = []
        for part, factors in zip(work[1:], columns[1:]):
            for j in range(step):
                part = part - factors[j] * pivots[j]
            done.append(part)
        done.append(jnp.concatenate(pivots, axis=0))
        return tuple(pltpu.roll(part, 2 * rank - step, axis=1) for part in done)

    parts = tuple(work[step * i : step * (i + 1)] for i in range(count))
    parts = lax.fori_loop(0, count, eliminate, parts)
    return jnp.concatenate(parts, axis=0)[:, :rank]


def solve(gram, left):
    solved = jnp.dot(
        left, inverse(gram) * (1.0 / groups), precision=exact, preferred_element_type=f32
    )
    high, low = split(solved, 2)
    return jnp.concatenate([high, high, low], axis=1)


def block_copy(k, offset, held, new_error, sems):
    begin = pl.multiple_of((2 * k + offset) * narrow, narrow)
    return pltpu.make_async_copy(held.at[k], new_error.at[:, pl.ds(begin, narrow)], sems.at[k])


def approx_block(k, factor, right):
    tiles = []
    for t in range(5):
        part = pl.ds(16 * t, 16)
        tiles.append(jnp.concatenate([right[8 * x + k, part, :] for x in range(4)], axis=0))
    high, low = split(jnp.concatenate(tiles, axis=1), 2)
    return dot(factor, jnp.concatenate([high, low, high], axis=0))


def own_kernel(
    gram, left, right, merged, weights, momentum, new_error, new_weights, new_momentum, factor,
    held, held_weights, held_momentum, sems, state_sems,
):
    core, z = lax.axis_index("core"), line_index()
    state = [
        pltpu.make_async_copy(held_weights, new_weights, state_sems.at[0]),
        pltpu.make_async_copy(held_momentum, new_momentum, state_sems.at[1]),
    ]
    factor[...] = solve(gram[...], left[...])

    approx = approx_block(z, factor[...], right)
    moved = momentum_decay * momentum[...] + approx
    held_momentum[...] = moved
    held_weights[...] = weights[...] - outer_rate * (approx + momentum_decay * moved)
    for copy in state:
        copy.start()

    for k in range(blocks):
        held[k] = (merged[k] - approx_block(k, factor[...], right)).astype(bf16)
        block_copy(k, core, held, new_error, sems).start()

    @pl.loop(0, blocks)
    def _(k):
        block_copy(k, core, held, new_error, sems).wait()

    for copy in state:
        copy.wait()


def finish_own(gram, left, right, merged, weights, momentum):
    return call(
        own_kernel, "own", 16, 16_000_000,
        in_specs=[vmem] * 6,
        out_specs=[hbm, hbm, hbm, vmem],
        out_shape=[
            shape(rows, cols, dtype=bf16),
            shape(rows, narrow),
            shape(rows, narrow),
            shape(rows, 3 * rank, dtype=bf16),
        ],
        scratch_shapes=[
            pltpu.VMEM((blocks, rows, narrow), bf16),
            pltpu.VMEM((rows, narrow), f32),
            pltpu.VMEM((rows, narrow), f32),
            pltpu.SemaphoreType.DMA((blocks,)),
            pltpu.SemaphoreType.DMA((2,)),
        ],
    )(gram, left, right, merged, weights, momentum)


def other_kernel(factor, right, merged, partial, new_error, held, sems):
    offset = 1 - lax.axis_index("core")

    for k in range(blocks):
        held[k] = (merged[k] - approx_block(k, factor[...], right)).astype(bf16)
        block_copy(k, offset, held, new_error, sems).start()

    @pl.loop(0, blocks)
    def _(k):
        block_copy(k, offset, held, new_error, sems).wait()


def finish_other(factor, right, merged, partial):
    return call(
        other_kernel, "other", 16, 8_000_000,
        in_specs=[vmem, vmem, vmem, hbm],
        out_specs=hbm,
        out_shape=shape(rows, cols, dtype=bf16),
        input_output_aliases={3: 0},
        scratch_shapes=[
            pltpu.VMEM((blocks, rows, narrow), bf16),
            pltpu.SemaphoreType.DMA((blocks,)),
        ],
    )(factor, right, merged, partial)


def swap(value):
    return lax.ppermute(value, "core", [(0, 1), (1, 0)])


def local(drift, error, start, weights, momentum):
    mine, theirs, keep, send = left_factor(drift[0], error[0], start.T)
    theirs, send = lax.optimization_barrier((swap(theirs), send))
    received = swap(send)
    mine = lax.all_to_all(pair_sum(mine, theirs), ("zh", "zl"), 0, 0)
    chunks, left = right_factor(mine, swap(mine), keep, received)
    plane = plane_sum(lax.all_to_all(chunks, ("x", "y", "zl"), 0, 0))
    line, gram = line_sum(lax.all_to_all(plane, "zh", 0, 0))
    own = lax.all_to_all(line, ("x", "y", "zl"), 0, 0)
    other = swap(own)
    partial, new_weights, new_momentum, factor = finish_own(
        gram, left, own, keep, weights, momentum
    )
    new_error = finish_other(factor, other, send, partial)
    return new_weights, new_error[None], new_momentum


def solution(mesh):
    fine = Mesh(mesh.devices.reshape(4, 2, 2, 4, 4), ("zh", "zl", "core", "x", "y"))
    replica, fsdp = ("zh", "zl", "core"), ("x", "y")
    return jax.shard_map(
        local,
        mesh=fine,
        in_specs=(
            P(replica, fsdp, None),
            P(replica, fsdp, None),
            P(),
            P(fsdp, replica),
            P(fsdp, replica),
        ),
        out_specs=(P(fsdp, replica), P(replica, fsdp, None), P(fsdp, replica)),
        check_vma=False,
    )
```

```python
import jax
import jax.numpy as jnp
from jax import lax
from jax.experimental import pallas as pl
from jax.experimental.pallas import tpu as pltpu
from jax.sharding import Mesh, PartitionSpec as P

outer_rate = 0.7
momentum_decay = 0.9

rows = 160
cols = 10240
rank = 64
narrow = 640
wide = 1280
blocks = 8
groups = 16
tall = 80
reads = 4
chunk = cols // reads
f32 = jnp.float32
bf16 = jnp.bfloat16
exact = lax.Precision.HIGHEST
mib = 1024 * 1024
around = ("zl", "x", "y")
hbm = pl.BlockSpec(memory_space=pltpu.HBM)
vmem = pl.BlockSpec(memory_space=pltpu.VMEM)


def split(value, pieces):
    out = []
    for _ in range(pieces - 1):
        head = value.astype(bf16)
        out.append(head)
        value = value - head.astype(f32)
    out.append(value.astype(bf16))
    return out


def dot(a, b):
    return jnp.dot(a, b, preferred_element_type=f32)


def dot_rows(a, b):
    return lax.dot_general(a, b, (((1,), (1,)), ((), ())), preferred_element_type=f32)


def call(kernel, name, size, moved, **kwargs):
    return pl.pallas_call(
        kernel,
        name=name,
        compiler_params=pltpu.CompilerParams(vmem_limit_bytes=size * mib),
        cost_estimate=pl.CostEstimate(flops=0, bytes_accessed=moved, transcendentals=0),
        **kwargs,
    )


def shape(*dims, dtype=f32):
    return jax.ShapeDtypeStruct(dims, dtype)


def pack(value):
    count = value.shape[0] // 2
    return jnp.concatenate([value[:count], value[count:]], axis=1)


def unpack(value):
    return jnp.concatenate([value[:, :rank], value[:, rank:]], axis=0)


def left_kernel(drift, error, start, mine, theirs, keep, send, drifts, errors, starts, acc, sems):
    first = lax.axis_index("core") == 0

    def copies(i):
        lanes = pl.ds(pl.multiple_of(i * chunk, chunk), chunk)
        return [
            pltpu.make_async_copy(start.at[:, lanes], starts.at[i], sems.at[i, 0]),
            pltpu.make_async_copy(drift.at[:, lanes], drifts.at[i], sems.at[i, 1]),
            pltpu.make_async_copy(error.at[:, lanes], errors.at[i], sems.at[i, 2]),
        ]

    for i in range(reads):
        for copy in copies(i):
            copy.start()
    acc[...] = jnp.zeros_like(acc)

    @pl.loop(0, reads)
    def _(i):
        for copy in copies(i):
            copy.wait()
        first_part, second_part = drifts[i], errors[i]
        merged = first_part.astype(f32) + second_part.astype(f32)
        both = jnp.concatenate([first_part, second_part], axis=0)
        acc[...] += dot_rows(both, jnp.concatenate(split(starts[i], 2), axis=0))
        for j in range(chunk // wide):
            even = merged[:, wide * j : wide * j + narrow]
            odd = merged[:, wide * j + narrow : wide * (j + 1)]
            k = i * (chunk // wide) + j
            keep[k] = jnp.where(first, even, odd)
            send[k] = jnp.where(first, odd, even)
    total = acc[:rows, :] + acc[rows:, :]
    left = total[:, :rank] + total[:, rank:]
    upper, lower = pack(left[: rows // 2]), pack(left[rows // 2 :])
    mine[...] = jnp.where(first, upper, lower)
    theirs[...] = jnp.where(first, lower, upper)


def left_factor(drift, error, start):
    inputs = [pltpu.with_memory_space_constraint(v, pltpu.HBM) for v in (drift, error, start)]
    return call(
        left_kernel, "left", 24, 13_000_000,
        in_specs=[hbm, hbm, hbm],
        out_specs=[vmem] * 4,
        out_shape=[
            pltpu.VMEM((rows // 4, 2 * rank), f32),
            pltpu.VMEM((rows // 4, 2 * rank), f32),
            pltpu.VMEM((blocks, rows, narrow), f32),
            pltpu.VMEM((blocks, rows, narrow), f32),
        ],
        scratch_shapes=[
            pltpu.VMEM((reads, rows, chunk), bf16),
            pltpu.VMEM((reads, rows, chunk), bf16),
            pltpu.VMEM((reads, rank, chunk), f32),
            pltpu.VMEM((2 * rows, 2 * rank), f32),
            pltpu.SemaphoreType.DMA((reads, 3)),
        ],
    )(*inputs)


def pair_sum_kernel(mine, received, out):
    total = mine[...] + received[...]
    for z in range(8):
        out[z] = total


def pair_sum(mine, received):
    return call(
        pair_sum_kernel, "pair_sum", 4, 500_000,
        in_specs=[vmem, vmem],
        out_specs=vmem,
        out_shape=shape(8, rows // 4, 2 * rank),
    )(mine, received)


def member(x, k):
    return 16 * (k % 2) + 4 * x + (k // 2)


def line_index():
    return 2 * lax.axis_index("zh") + lax.axis_index("zl")


def right_kernel(mine, theirs, keep, received, out, left_out, gram):
    own = unpack(jnp.sum(mine[...], axis=0)) * (1.0 / groups)
    other = unpack(jnp.sum(theirs[...], axis=0)) * (1.0 / groups)
    first = lax.axis_index("core") == 0
    left = jnp.concatenate([jnp.where(first, own, other), jnp.where(first, other, own)], axis=0)
    left_out[...] = left
    turned = left.T
    pieces = jnp.concatenate(split(turned, 3), axis=0)
    gram[...] = jnp.dot(turned, left, precision=exact, preferred_element_type=f32)
    share = gram[pl.ds(pl.multiple_of(line_index() * 8, 8), 8), :]
    empty = jnp.zeros((8, rank), f32)
    even = lax.axis_index("zl") == 0
    padded = jnp.concatenate(
        [jnp.where(even, share, empty), jnp.where(even, empty, share)], axis=1
    )
    for j in range(32):
        out[j, tall:, :] = padded

    for k in range(blocks):
        high, low = split(keep[k] + received[k], 2)
        term = dot(pieces, high) + dot(pieces, low)
        block = term[:rank] + term[rank : 2 * rank] + term[2 * rank :]
        for x in range(4):
            for t in range(5):
                out[member(x, k), 16 * t : 16 * (t + 1), :] = block[
                    16 * x : 16 * (x + 1), 128 * t : 128 * (t + 1)
                ]


def right_factor(mine, theirs, keep, received):
    return call(
        right_kernel, "right", 16, 10_000_000,
        in_specs=[vmem] * 4,
        out_specs=[vmem, vmem],
        out_shape=[shape(32, tall + 8, 128), shape(rows, rank)],
        scratch_shapes=[pltpu.VMEM((rank, rank), f32)],
    )(mine, theirs, keep, received)


def plane_sum_kernel(chunks, out):
    total = chunks[0]
    for j in range(1, 32):
        total += chunks[j]
    for z in range(4):
        out[z] = total


def plane_sum(chunks):
    return call(
        plane_sum_kernel, "plane_sum", 8, 3_000_000,
        in_specs=[vmem],
        out_specs=vmem,
        out_shape=shape(4, tall + 8, 128),
    )(chunks)


def line_sum_kernel(chunks, out, gram):
    total = chunks[0, :tall, :]
    for j in range(1, 4):
        total += chunks[j, :tall, :]
    for j in range(32):
        out[j] = total
    for j in range(4):
        pair = chunks[j, tall:, :]
        gram[16 * j : 16 * j + 8, :] = pair
        gram[16 * j + 8 : 16 * (j + 1), :] = jnp.concatenate(
            [pair[:, rank:], pair[:, :rank]], axis=1
        )


def line_sum(chunks):
    return call(
        line_sum_kernel, "line_sum", 8, 3_000_000,
        in_specs=[vmem],
        out_specs=[vmem, vmem],
        out_shape=[shape(32, tall, 128), shape(rank, 2 * rank)],
    )(chunks)


def inverse(gram):
    size = (rank, 2 * rank)
    row = lax.broadcasted_iota(jnp.int32, size, 0)
    lane = lax.broadcasted_iota(jnp.int32, size, 1)
    work = jnp.where(lane < rank, gram, (lane == row + rank).astype(f32))
    step = 8
    count = rank // step

    def eliminate(_, work):
        columns = [
            [jnp.broadcast_to(part[:, j : j + 1], (step, 2 * rank)) for j in range(step)]
            for part in work
        ]
        block = [[columns[0][j][i : i + 1, :] for j in range(step)] for i in range(step)]
        pivots = [work[0][i : i + 1, :] for i in range(step)]
        for j in range(step):
            scale = 1.0 / block[j][j]
            pivots[j] = pivots[j] * scale
            for m in range(j + 1, step):
                block[j][m] = block[j][m] * scale
            for i in range(step):
                if i != j:
                    pivots[i] = pivots[i] - block[i][j] * pivots[j]
                    for m in range(j + 1, step):
                        block[i][m] = block[i][m] - block[i][j] * block[j][m]
        done = []
        for part, factors in zip(work[1:], columns[1:]):
            for j in range(step):
                part = part - factors[j] * pivots[j]
            done.append(part)
        done.append(jnp.concatenate(pivots, axis=0))
        return tuple(pltpu.roll(part, 2 * rank - step, axis=1) for part in done)

    parts = tuple(work[step * i : step * (i + 1)] for i in range(count))
    parts = lax.fori_loop(0, count, eliminate, parts)
    return jnp.concatenate(parts, axis=0)[:, :rank]


def solve(gram, left):
    solved = jnp.dot(
        left, inverse(gram) * (1.0 / groups), precision=exact, preferred_element_type=f32
    )
    high, low = split(solved, 2)
    return jnp.concatenate([high, high, low], axis=1)


def block_copy(k, offset, held, new_error, sems):
    begin = pl.multiple_of((2 * k + offset) * narrow, narrow)
    return pltpu.make_async_copy(held.at[k], new_error.at[:, pl.ds(begin, narrow)], sems.at[k])


def approx_block(k, factor, right):
    tiles = []
    for t in range(5):
        part = pl.ds(16 * t, 16)
        tiles.append(jnp.concatenate([right[member(x, k), part, :] for x in range(4)], axis=0))
    high, low = split(jnp.concatenate(tiles, axis=1), 2)
    return dot(factor, jnp.concatenate([high, low, high], axis=0))


def own_kernel(
    gram, left, right, merged, weights, momentum, new_error, new_weights, new_momentum, factor,
    held, held_weights, held_momentum, sems, state_sems,
):
    core, z = lax.axis_index("core"), line_index()
    state = [
        pltpu.make_async_copy(held_weights, new_weights, state_sems.at[0]),
        pltpu.make_async_copy(held_momentum, new_momentum, state_sems.at[1]),
    ]
    factor[...] = solve(gram[...], left[...])

    approx = approx_block(z, factor[...], right)
    moved = momentum_decay * momentum[...] + approx
    held_momentum[...] = moved
    held_weights[...] = weights[...] - outer_rate * (approx + momentum_decay * moved)
    for copy in state:
        copy.start()

    for k in range(blocks):
        held[k] = (merged[k] - approx_block(k, factor[...], right)).astype(bf16)
        block_copy(k, core, held, new_error, sems).start()

    @pl.loop(0, blocks)
    def _(k):
        block_copy(k, core, held, new_error, sems).wait()

    for copy in state:
        copy.wait()


def finish_own(gram, left, right, merged, weights, momentum):
    return call(
        own_kernel, "own", 16, 16_000_000,
        in_specs=[vmem] * 6,
        out_specs=[hbm, hbm, hbm, vmem],
        out_shape=[
            shape(rows, cols, dtype=bf16),
            shape(rows, narrow),
            shape(rows, narrow),
            shape(rows, 3 * rank, dtype=bf16),
        ],
        scratch_shapes=[
            pltpu.VMEM((blocks, rows, narrow), bf16),
            pltpu.VMEM((rows, narrow), f32),
            pltpu.VMEM((rows, narrow), f32),
            pltpu.SemaphoreType.DMA((blocks,)),
            pltpu.SemaphoreType.DMA((2,)),
        ],
    )(gram, left, right, merged, weights, momentum)


def other_kernel(factor, right, merged, partial, new_error, held, sems):
    offset = 1 - lax.axis_index("core")

    for k in range(blocks):
        held[k] = (merged[k] - approx_block(k, factor[...], right)).astype(bf16)
        block_copy(k, offset, held, new_error, sems).start()

    @pl.loop(0, blocks)
    def _(k):
        block_copy(k, offset, held, new_error, sems).wait()


def finish_other(factor, right, merged, partial):
    return call(
        other_kernel, "other", 16, 8_000_000,
        in_specs=[vmem, vmem, vmem, hbm],
        out_specs=hbm,
        out_shape=shape(rows, cols, dtype=bf16),
        input_output_aliases={3: 0},
        scratch_shapes=[
            pltpu.VMEM((blocks, rows, narrow), bf16),
            pltpu.SemaphoreType.DMA((blocks,)),
        ],
    )(factor, right, merged, partial)


def swap(value):
    return lax.ppermute(value, "core", [(0, 1), (1, 0)])


def local(drift, error, start, weights, momentum):
    mine, theirs, keep, send = left_factor(drift[0], error[0], start.T)
    theirs, send = lax.optimization_barrier((swap(theirs), send))
    received = swap(send)
    mine = lax.all_to_all(pair_sum(mine, theirs), ("zh", "zl"), 0, 0)
    chunks, left = right_factor(mine, swap(mine), keep, received)
    plane = plane_sum(lax.all_to_all(chunks, around, 0, 0))
    line, gram = line_sum(lax.all_to_all(plane, "zh", 0, 0))
    own = lax.all_to_all(line, around, 0, 0)
    other = swap(own)
    partial, new_weights, new_momentum, factor = finish_own(
        gram, left, own, keep, weights, momentum
    )
    new_error = finish_other(factor, other, send, partial)
    return new_weights, new_error[None], new_momentum


def solution(mesh):
    fine = Mesh(mesh.devices.reshape(4, 2, 2, 4, 4), ("zh", "zl", "core", "x", "y"))
    replica, fsdp = ("zh", "zl", "core"), ("x", "y")
    return jax.shard_map(
        local,
        mesh=fine,
        in_specs=(
            P(replica, fsdp, None),
            P(replica, fsdp, None),
            P(),
            P(fsdp, replica),
            P(fsdp, replica),
        ),
        out_specs=(P(fsdp, replica), P(replica, fsdp, None), P(fsdp, replica)),
        check_vma=False,
    )
```

```python
import jax
import jax.numpy as jnp
from jax import lax
from jax.experimental import pallas as pl
from jax.experimental.pallas import tpu as pltpu
from jax.sharding import Mesh, PartitionSpec as P

outer_rate = 0.7
momentum_decay = 0.9

rows = 160
cols = 10240
rank = 64
narrow = 640
wide = 1280
blocks = 8
groups = 16
tall = 80
reads = 4
chunk = cols // reads
f32 = jnp.float32
bf16 = jnp.bfloat16
exact = lax.Precision.HIGHEST
mib = 1024 * 1024
around = ("zl", "x", "y")
hbm = pl.BlockSpec(memory_space=pltpu.HBM)
vmem = pl.BlockSpec(memory_space=pltpu.VMEM)


def split(value, pieces):
    out = []
    for _ in range(pieces - 1):
        head = value.astype(bf16)
        out.append(head)
        value = value - head.astype(f32)
    out.append(value.astype(bf16))
    return out


def dot(a, b):
    return jnp.dot(a, b, preferred_element_type=f32)


def dot_rows(a, b):
    return lax.dot_general(a, b, (((1,), (1,)), ((), ())), preferred_element_type=f32)


def call(kernel, name, size, moved, **kwargs):
    return pl.pallas_call(
        kernel,
        name=name,
        compiler_params=pltpu.CompilerParams(vmem_limit_bytes=size * mib),
        cost_estimate=pl.CostEstimate(flops=0, bytes_accessed=moved, transcendentals=0),
        **kwargs,
    )


def shape(*dims, dtype=f32):
    return jax.ShapeDtypeStruct(dims, dtype)


def pack(value):
    count = value.shape[0] // 2
    return jnp.concatenate([value[:count], value[count:]], axis=1)


def unpack(value):
    return jnp.concatenate([value[:, :rank], value[:, rank:]], axis=0)


def left_kernel(drift, error, start, mine, theirs, keep, send, drifts, errors, starts, acc, sems):
    first = lax.axis_index("core") == 0

    def copies(i):
        lanes = pl.ds(pl.multiple_of(i * chunk, chunk), chunk)
        return [
            pltpu.make_async_copy(start.at[:, lanes], starts.at[i], sems.at[i, 0]),
            pltpu.make_async_copy(drift.at[:, lanes], drifts.at[i], sems.at[i, 1]),
            pltpu.make_async_copy(error.at[:, lanes], errors.at[i], sems.at[i, 2]),
        ]

    for i in range(reads):
        for copy in copies(i):
            copy.start()
    acc[...] = jnp.zeros_like(acc)

    @pl.loop(0, reads)
    def _(i):
        for copy in copies(i):
            copy.wait()
        first_part, second_part = drifts[i], errors[i]
        merged = first_part.astype(f32) + second_part.astype(f32)
        both = jnp.concatenate([first_part, second_part], axis=0)
        acc[...] += dot_rows(both, jnp.concatenate(split(starts[i], 2), axis=0))
        for j in range(chunk // wide):
            even = merged[:, wide * j : wide * j + narrow]
            odd = merged[:, wide * j + narrow : wide * (j + 1)]
            k = i * (chunk // wide) + j
            keep[k] = jnp.where(first, even, odd)
            send[k] = jnp.where(first, odd, even)
    total = acc[:rows, :] + acc[rows:, :]
    left = total[:, :rank] + total[:, rank:]
    upper, lower = pack(left[: rows // 2]), pack(left[rows // 2 :])
    mine[...] = jnp.where(first, upper, lower)
    theirs[...] = jnp.where(first, lower, upper)


def left_factor(drift, error, start):
    inputs = [pltpu.with_memory_space_constraint(v, pltpu.HBM) for v in (drift, error, start)]
    return call(
        left_kernel, "left", 24, 13_000_000,
        in_specs=[hbm, hbm, hbm],
        out_specs=[vmem] * 4,
        out_shape=[
            pltpu.VMEM((rows // 4, 2 * rank), f32),
            pltpu.VMEM((rows // 4, 2 * rank), f32),
            pltpu.VMEM((blocks, rows, narrow), f32),
            pltpu.VMEM((blocks, rows, narrow), f32),
        ],
        scratch_shapes=[
            pltpu.VMEM((reads, rows, chunk), bf16),
            pltpu.VMEM((reads, rows, chunk), bf16),
            pltpu.VMEM((reads, rank, chunk), f32),
            pltpu.VMEM((2 * rows, 2 * rank), f32),
            pltpu.SemaphoreType.DMA((reads, 3)),
        ],
    )(*inputs)


def pair_sum_kernel(mine, received, out):
    total = mine[...] + received[...]
    for z in range(8):
        out[z] = total


def pair_sum(mine, received):
    return call(
        pair_sum_kernel, "pair_sum", 4, 500_000,
        in_specs=[vmem, vmem],
        out_specs=vmem,
        out_shape=shape(8, rows // 4, 2 * rank),
    )(mine, received)


def member(x, k):
    return 16 * (k % 2) + 4 * x + (k // 2)


def line_index():
    return 2 * lax.axis_index("zh") + lax.axis_index("zl")


def right_kernel(mine, theirs, keep, received, out, left_out, gram):
    own = unpack(jnp.sum(mine[...], axis=0)) * (1.0 / groups)
    other = unpack(jnp.sum(theirs[...], axis=0)) * (1.0 / groups)
    first = lax.axis_index("core") == 0
    left = jnp.concatenate([jnp.where(first, own, other), jnp.where(first, other, own)], axis=0)
    left_out[...] = left
    turned = left.T
    pieces = jnp.concatenate(split(turned, 3), axis=0)
    gram[...] = jnp.dot(turned, left, precision=exact, preferred_element_type=f32)
    share = gram[pl.ds(pl.multiple_of(line_index() * 8, 8), 8), :]
    empty = jnp.zeros((8, rank), f32)
    even = lax.axis_index("zl") == 0
    padded = jnp.concatenate(
        [jnp.where(even, share, empty), jnp.where(even, empty, share)], axis=1
    )
    for j in range(32):
        out[j, tall:, :] = padded

    for k in range(blocks):
        high, low = split(keep[k] + received[k], 2)
        term = dot(pieces, high) + dot(pieces, low)
        block = term[:rank] + term[rank : 2 * rank] + term[2 * rank :]
        for x in range(4):
            for t in range(5):
                out[member(x, k), 16 * t : 16 * (t + 1), :] = block[
                    16 * x : 16 * (x + 1), 128 * t : 128 * (t + 1)
                ]


def right_factor(mine, theirs, keep, received):
    return call(
        right_kernel, "right", 16, 10_000_000,
        in_specs=[vmem] * 4,
        out_specs=[vmem, vmem],
        out_shape=[shape(32, tall + 8, 128), shape(rows, rank)],
        scratch_shapes=[pltpu.VMEM((rank, rank), f32)],
    )(mine, theirs, keep, received)


def plane_sum_kernel(chunks, out):
    total = chunks[0]
    for j in range(1, 32):
        total += chunks[j]
    for z in range(4):
        out[z] = total


def plane_sum(chunks):
    return call(
        plane_sum_kernel, "plane_sum", 8, 3_000_000,
        in_specs=[vmem],
        out_specs=vmem,
        out_shape=shape(4, tall + 8, 128),
    )(chunks)


def line_sum_kernel(chunks, out, gram):
    total = chunks[0, :tall, :]
    for j in range(1, 4):
        total += chunks[j, :tall, :]
    for j in range(32):
        out[j] = total
    for j in range(4):
        pair = chunks[j, tall:, :]
        gram[16 * j : 16 * j + 8, :] = pair
        gram[16 * j + 8 : 16 * (j + 1), :] = jnp.concatenate(
            [pair[:, rank:], pair[:, :rank]], axis=1
        )


def line_sum(chunks):
    return call(
        line_sum_kernel, "line_sum", 8, 3_000_000,
        in_specs=[vmem],
        out_specs=[vmem, vmem],
        out_shape=[shape(32, tall, 128), shape(rank, 2 * rank)],
    )(chunks)


def inverse(gram):
    size = (rank, 2 * rank)
    row = lax.broadcasted_iota(jnp.int32, size, 0)
    lane = lax.broadcasted_iota(jnp.int32, size, 1)
    work = jnp.where(lane < rank, gram, (lane == row + rank).astype(f32))
    step = 8
    count = rank // step

    def eliminate(_, work):
        columns = [
            [jnp.broadcast_to(part[:, j : j + 1], (step, 2 * rank)) for j in range(step)]
            for part in work
        ]
        block = [[columns[0][j][i : i + 1, :] for j in range(step)] for i in range(step)]
        pivots = [work[0][i : i + 1, :] for i in range(step)]
        for j in range(step):
            scale = pl.reciprocal(block[j][j], approx=False)
            pivots[j] = pivots[j] * scale
            for m in range(j + 1, step):
                block[j][m] = block[j][m] * scale
            for i in range(step):
                if i != j:
                    pivots[i] = pivots[i] - block[i][j] * pivots[j]
                    for m in range(j + 1, step):
                        block[i][m] = block[i][m] - block[i][j] * block[j][m]
        done = []
        for part, factors in zip(work[1:], columns[1:]):
            for j in range(step):
                part = part - factors[j] * pivots[j]
            done.append(part)
        done.append(jnp.concatenate(pivots, axis=0))
        return tuple(pltpu.roll(part, 2 * rank - step, axis=1) for part in done)

    parts = tuple(work[step * i : step * (i + 1)] for i in range(count))
    parts = lax.fori_loop(0, count, eliminate, parts)
    return jnp.concatenate(parts, axis=0)[:, :rank]


def solve(gram, left):
    solved = jnp.dot(
        left, inverse(gram) * (1.0 / groups), precision=exact, preferred_element_type=f32
    )
    high, low = split(solved, 2)
    return jnp.concatenate([high, high, low], axis=1)


def block_copy(k, offset, held, new_error, sems):
    begin = pl.multiple_of((2 * k + offset) * narrow, narrow)
    return pltpu.make_async_copy(held.at[k], new_error.at[:, pl.ds(begin, narrow)], sems.at[k])


def approx_block(k, factor, right):
    tiles = []
    for t in range(5):
        part = pl.ds(16 * t, 16)
        tiles.append(jnp.concatenate([right[member(x, k), part, :] for x in range(4)], axis=0))
    high, low = split(jnp.concatenate(tiles, axis=1), 2)
    return dot(factor, jnp.concatenate([high, low, high], axis=0))


def own_kernel(
    gram, left, right, merged, weights, momentum, new_error, new_weights, new_momentum, factor,
    held, held_weights, held_momentum, sems, state_sems,
):
    core, z = lax.axis_index("core"), line_index()
    state = [
        pltpu.make_async_copy(held_weights, new_weights, state_sems.at[0]),
        pltpu.make_async_copy(held_momentum, new_momentum, state_sems.at[1]),
    ]
    factor[...] = solve(gram[...], left[...])

    approx = approx_block(z, factor[...], right)
    moved = momentum_decay * momentum[...] + approx
    held_momentum[...] = moved
    held_weights[...] = weights[...] - outer_rate * (approx + momentum_decay * moved)
    for copy in state:
        copy.start()

    for k in range(blocks):
        held[k] = (merged[k] - approx_block(k, factor[...], right)).astype(bf16)
        block_copy(k, core, held, new_error, sems).start()

    @pl.loop(0, blocks)
    def _(k):
        block_copy(k, core, held, new_error, sems).wait()

    for copy in state:
        copy.wait()


def finish_own(gram, left, right, merged, weights, momentum):
    return call(
        own_kernel, "own", 16, 16_000_000,
        in_specs=[vmem] * 6,
        out_specs=[hbm, hbm, hbm, vmem],
        out_shape=[
            shape(rows, cols, dtype=bf16),
            shape(rows, narrow),
            shape(rows, narrow),
            shape(rows, 3 * rank, dtype=bf16),
        ],
        scratch_shapes=[
            pltpu.VMEM((blocks, rows, narrow), bf16),
            pltpu.VMEM((rows, narrow), f32),
            pltpu.VMEM((rows, narrow), f32),
            pltpu.SemaphoreType.DMA((blocks,)),
            pltpu.SemaphoreType.DMA((2,)),
        ],
    )(gram, left, right, merged, weights, momentum)


def other_kernel(factor, right, merged, partial, new_error, held, sems):
    offset = 1 - lax.axis_index("core")

    for k in range(blocks):
        held[k] = (merged[k] - approx_block(k, factor[...], right)).astype(bf16)
        block_copy(k, offset, held, new_error, sems).start()

    @pl.loop(0, blocks)
    def _(k):
        block_copy(k, offset, held, new_error, sems).wait()


def finish_other(factor, right, merged, partial):
    return call(
        other_kernel, "other", 16, 8_000_000,
        in_specs=[vmem, vmem, vmem, hbm],
        out_specs=hbm,
        out_shape=shape(rows, cols, dtype=bf16),
        input_output_aliases={3: 0},
        scratch_shapes=[
            pltpu.VMEM((blocks, rows, narrow), bf16),
            pltpu.SemaphoreType.DMA((blocks,)),
        ],
    )(factor, right, merged, partial)


def swap(value):
    return lax.ppermute(value, "core", [(0, 1), (1, 0)])


def local(drift, error, start, weights, momentum):
    mine, theirs, keep, send = left_factor(drift[0], error[0], start.T)
    theirs, send = lax.optimization_barrier((swap(theirs), send))
    received = swap(send)
    mine = lax.all_to_all(pair_sum(mine, theirs), ("zh", "zl"), 0, 0)
    chunks, left = right_factor(mine, swap(mine), keep, received)
    plane = plane_sum(lax.all_to_all(chunks, around, 0, 0))
    line, gram = line_sum(lax.all_to_all(plane, "zh", 0, 0))
    own = lax.all_to_all(line, around, 0, 0)
    other = swap(own)
    partial, new_weights, new_momentum, factor = finish_own(
        gram, left, own, keep, weights, momentum
    )
    new_error = finish_other(factor, other, send, partial)
    return new_weights, new_error[None], new_momentum


def solution(mesh):
    fine = Mesh(mesh.devices.reshape(4, 2, 2, 4, 4), ("zh", "zl", "core", "x", "y"))
    replica, fsdp = ("zh", "zl", "core"), ("x", "y")
    return jax.shard_map(
        local,
        mesh=fine,
        in_specs=(
            P(replica, fsdp, None),
            P(replica, fsdp, None),
            P(),
            P(fsdp, replica),
            P(fsdp, replica),
        ),
        out_specs=(P(fsdp, replica), P(replica, fsdp, None), P(fsdp, replica)),
        check_vma=False,
    )
```
